32 devices in a mesh: grp: 1, strip: 4 (over z), col: 4 (over y, x), chan: 2 (over core).
Axes of the slice: x: 2, y: 2, z: 4, core: 2. Of those that a mesh axis runs over, the one named last changes fastest.
Arguments:
- features: bfloat16 [64, 128, 256], P(('grp', 'strip'), 'col', 'chan'), may hold values from -6 to 6
- tile_first: bfloat16 [3, 3, 256, 256], P(None, None, None, 'chan'), may hold values from -0.125 to 0.125
- tile_second: bfloat16 [3, 3, 256, 256], P(None, None, None, 'chan'), may hold values from -0.125 to 0.125
- mask_first: bfloat16 [3, 3, 256, 256], P(None, None, None, 'chan'), may hold values from -0.125 to 0.125
- mask_second: bfloat16 [3, 3, 256, 256], P(None, None, None, 'chan'), may hold values from -0.125 to 0.125
- region_boxes: int32 [4, 4, 12, 4], P(('grp', 'strip'), 'col'), may hold values from 0 to 124, as said below
- owner_strip: int32 [4, 4, 12], P(('grp', 'strip'), 'col'), may hold values from 0 to 3, as said below
- cotangent: bfloat16 [4, 4, 15, 14, 14, 256], P(('grp', 'strip'), 'col', None, None, None, 'chan'), may hold values from -6 to 6
Outputs:
- mask_features: bfloat16 [4, 4, 15, 14, 14, 256], P(('grp', 'strip'), 'col', None, None, None, 'chan')
- grad_features: bfloat16 [64, 128, 256], P(('grp', 'strip'), 'col', 'chan')
The draws below stay inside these ranges and needn't reach their ends.
Inputs may be any that keep to these rules, and one draw needn't show every extreme that they name: `region_boxes`: each box lies inside the tile of the strip and column where it is listed: rows from s * 16 to s * 16 + 15 for strip s, columns likewise with 32; height 4 to 16, width 4 to 32. `owner_strip`: in each column, a quarter of the strips own 15 regions, half own 12, a quarter own 2 * 12 - 15 (which ones varies); so an owner holds at most 15 regions and one tile sends at most 4 of its regions to one owner, both reached. Numbering the regions of a column by q * 4 + s, each owner's regions form one run in this numbering, taken cyclically.
All inputs are finite; a program needn't handle non-finite values.
Results may differ from the reference program's by a relative error of at most 0.017.
Values may be sent and summed in bfloat16 or wider, within the bound.
A program may use at most 128 MiB of HBM per device.

```python
import jax
import jax.numpy as jnp
from jax import lax

C = 256
BLOCK = 14
ROWS = 16
COLS = 32
SLOTS = 12
RECV = 15
H = 64
W = 128
N_STRIP = 4
N_COL = 4
N_CHAN = 2


def draw_region_boxes(key, part):
    key = jax.random.fold_in(key, 23)
    height_key, width_key, top_key, left_key = jax.random.split(key, 4)
    shape_all = (N_STRIP, N_COL, SLOTS)
    heights = jax.random.randint(height_key, shape_all, 4, ROWS + 1)
    widths = jax.random.randint(width_key, shape_all, 4, COLS + 1)
    strip_base = (jnp.arange(N_STRIP, dtype=jnp.int32) * ROWS)[:, None, None]
    col_base = (jnp.arange(N_COL, dtype=jnp.int32) * COLS)[None, :, None]
    top_rows = strip_base + jax.random.randint(top_key, shape_all, 0, ROWS - heights + 1)
    left_cols = col_base + jax.random.randint(left_key, shape_all, 0, COLS - widths + 1)
    top_rows = top_rows.at[0, 0, 0].set(0)
    left_cols = left_cols.at[0, 0, 0].set(0)
    heights = heights.at[N_STRIP - 1, N_COL - 1, 0].set(4)
    widths = widths.at[N_STRIP - 1, N_COL - 1, 0].set(4)
    top_rows = top_rows.at[N_STRIP - 1, N_COL - 1, 0].set(N_STRIP * ROWS - 4)
    left_cols = left_cols.at[N_STRIP - 1, N_COL - 1, 0].set(N_COL * COLS - 4)
    return jnp.stack([top_rows, left_cols, heights, widths], axis=-1).astype(jnp.int32)


def draw_owner_strip(key, part):
    key = jax.random.fold_in(key, 11)
    tickets_all = N_STRIP * SLOTS
    quarter = N_STRIP // 4
    extra = SLOTS // 4
    position = jnp.arange(N_STRIP, dtype=jnp.int32)
    owner_loads = jnp.where(position < quarter, SLOTS + extra, jnp.where(position < 3 * quarter, SLOTS, SLOTS - extra))
    load_ends = jnp.cumsum(owner_loads)

    def one_column(col_key):
        order_key, rotate_key = jax.random.split(col_key)
        ordering = jax.random.permutation(order_key, N_STRIP)
        rotation = jax.random.randint(rotate_key, (), 0, tickets_all)
        tickets = (jnp.arange(SLOTS, dtype=jnp.int32)[None, :] * N_STRIP + jnp.arange(N_STRIP, dtype=jnp.int32)[:, None] + rotation) % tickets_all
        position_of = jnp.sum((load_ends[None, None, :] <= tickets[:, :, None]).astype(jnp.int32), axis=2)
        return ordering[position_of]
    columns = jax.vmap(one_column)(jax.random.split(key, N_COL))
    return jnp.transpose(columns, (1, 0, 2)).astype(jnp.int32)


def block_levels(own_key, dims, cuts, low, high):
    gain = 1.0
    for dim, blocks in cuts:
        draws = jax.random.uniform(jax.random.fold_in(jax.random.fold_in(own_key, 6), dim), (blocks,), jnp.float32, low / len(cuts), high / len(cuts))
        gain = gain * jnp.repeat(jnp.exp(draws), dims[dim] // blocks).reshape((-1,) + (1,) * (len(dims) - 1 - dim))
    return gain


def bell_draw(stream_key, dims, scale, reach, cuts=(), kind=jnp.bfloat16):
    drawn = scale * jax.random.normal(stream_key, dims, jnp.float32)
    if cuts:
        drawn = drawn * block_levels(stream_key, dims, cuts, -0.22, 0.18)
    return jnp.clip(drawn, -reach, reach).astype(kind)


def setup_inputs(seed: int = 0, part: int = 0) -> dict:
    seeds = jax.random.split(jax.random.key(seed), 9)
    own_keys = jax.random.split(jax.random.fold_in(seeds[8], part), 9)
    features = bell_draw(own_keys[0], (H, W, C), 1.0, 6.0, ((0, 4), (1, 4), (2, 2)))
    tile_first = bell_draw(seeds[1], (3, 3, C, C), (9 * C) ** -0.5, 0.125, ((3, 2),))
    tile_second = bell_draw(seeds[2], (3, 3, C, C), (9 * C) ** -0.5, 0.125, ((3, 2),))
    mask_first = bell_draw(seeds[3], (3, 3, C, C), (9 * C) ** -0.5, 0.125, ((3, 2),))
    mask_second = bell_draw(seeds[4], (3, 3, C, C), (9 * C) ** -0.5, 0.125, ((3, 2),))
    region_boxes = draw_region_boxes(jax.random.fold_in(jax.random.fold_in(seeds[8], part), 71), part)
    owner_strip = draw_owner_strip(jax.random.fold_in(jax.random.fold_in(seeds[8], part), 71), part)
    cotangent = bell_draw(own_keys[7], (N_STRIP, N_COL, RECV, BLOCK, BLOCK, C), 1.0, 6.0, ((0, 4), (1, 4), (5, 2)))
    return {"features": features, "tile_first": tile_first, "tile_second": tile_second, "mask_first": mask_first, "mask_second": mask_second, "region_boxes": region_boxes, "owner_strip": owner_strip, "cotangent": cotangent}


def correlate(inputs, weight):
    return lax.conv_general_dilated(inputs.astype(jnp.float32), weight.astype(jnp.float32), (1, 1), "SAME", dimension_numbers=("NHWC", "HWIO", "NHWC"), precision=lax.Precision.HIGHEST)


def silu_slope(pre_act):
    sigmoid_v = jax.nn.sigmoid(pre_act)
    return sigmoid_v * (1.0 + pre_act * (1.0 - sigmoid_v))


def correlate_back(grad_map, weight):
    half_width = C // N_CHAN
    accum = jnp.zeros(grad_map.shape[:-1] + (C,), jnp.float32)
    for half_index in range(N_CHAN):
        piece = grad_map[..., half_index * half_width:(half_index + 1) * half_width]
        flipped = jnp.flip(weight[..., half_index * half_width:(half_index + 1) * half_width], (0, 1)).transpose(0, 1, 3, 2)
        partial_value = correlate(piece, flipped).astype(jnp.bfloat16)
        partial_value = lax.optimization_barrier(partial_value)
        accum = accum + partial_value.astype(jnp.float32)
    return accum


def bilinear(start_at, length, anchor, cells, samples):
    sample_ids = jnp.arange(samples, dtype=jnp.int32)
    twice = 2 * samples
    numerator = twice * start_at[..., None] + (2 * sample_ids + 1) * length[..., None] - samples
    last_cell = (start_at + length - 1)[..., None]
    numerator = jnp.minimum(jnp.maximum(numerator, twice * start_at[..., None]), twice * last_cell)
    near_low = numerator // twice
    fraction = (numerator - twice * near_low).astype(jnp.float32) / twice
    near_high = jnp.minimum(near_low + 1, last_cell)
    positions = jnp.asarray(anchor, jnp.int32)[..., None, None] + jnp.arange(cells, dtype=jnp.int32)
    lower_part = jnp.where(positions == near_low[..., None], (1.0 - fraction)[..., None], jnp.float32(0.0))
    upper_part = jnp.where(positions == near_high[..., None], fraction[..., None], jnp.float32(0.0))
    return lower_part + upper_part


def reference(features, tile_first, tile_second, mask_first, mask_second, region_boxes, owner_strip, cotangent):
    hidden = jax.nn.silu(correlate(features[None], tile_first))[0].astype(jnp.bfloat16)
    feat = jax.nn.silu(correlate(hidden[None], tile_second))[0].astype(jnp.bfloat16)
    tile_stack = feat.reshape(N_STRIP, ROWS, N_COL, COLS, C).transpose(0, 2, 1, 3, 4).astype(jnp.float32)
    anchor_rows = (jnp.arange(N_STRIP, dtype=jnp.int32) * ROWS)[:, None, None]
    anchor_cols = (jnp.arange(N_COL, dtype=jnp.int32) * COLS)[None, :, None]
    row_weight = bilinear(region_boxes[..., 0], region_boxes[..., 2], anchor_rows, ROWS, BLOCK)
    col_weight = bilinear(region_boxes[..., 1], region_boxes[..., 3], anchor_cols, COLS, BLOCK)
    partial_value = jnp.einsum("ncsiy,ncyxh->ncsixh", row_weight, tile_stack, precision=lax.Precision.HIGHEST)
    crop_blocks = jnp.einsum("ncskx,ncsixh->ncsikh", col_weight, partial_value, precision=lax.Precision.HIGHEST).astype(jnp.bfloat16)

    strip_ids = jnp.arange(N_STRIP, dtype=jnp.int32)
    owner_hits = (owner_strip[..., None] == strip_ids).astype(jnp.int32)
    arriving = jnp.sum(owner_hits, axis=2)
    before = jnp.cumsum(arriving, axis=0) - arriving
    slot_ids = jnp.arange(SLOTS, dtype=jnp.int32)
    earlier_same = (owner_strip[..., :, None] == owner_strip[..., None, :]) & (slot_ids[None, :] < slot_ids[:, None])
    pair_rank = jnp.sum(earlier_same.astype(jnp.int32), axis=-1)
    owner_slot = (jnp.take_along_axis(before, owner_strip, axis=2) + pair_rank).astype(jnp.int32)
    column_ids = jnp.broadcast_to(jnp.arange(N_COL, dtype=jnp.int32)[None, :, None], owner_strip.shape)

    region_count = N_STRIP * N_COL * SLOTS
    crops_flat = crop_blocks.reshape(region_count, BLOCK, BLOCK, C)
    cot_blocks = cotangent[owner_strip, column_ids, owner_slot].reshape(region_count, BLOCK, BLOCK, C)

    pre_one = correlate(crops_flat, mask_first)
    act_one = jax.nn.silu(pre_one).astype(jnp.bfloat16)
    pre_two = correlate(act_one, mask_second)
    masks_flat = jax.nn.silu(pre_two).astype(jnp.bfloat16)
    grad_two = (cot_blocks.astype(jnp.float32) * silu_slope(pre_two)).astype(jnp.bfloat16)
    grad_act = correlate_back(grad_two, mask_second)
    grad_one = (grad_act * silu_slope(pre_one)).astype(jnp.bfloat16)
    crop_grad = correlate_back(grad_one, mask_first).astype(jnp.bfloat16)

    mask_features = jnp.zeros((N_STRIP, N_COL, RECV, BLOCK, BLOCK, C), jnp.bfloat16)
    mask_features = mask_features.at[owner_strip, column_ids, owner_slot].set(masks_flat.reshape(N_STRIP, N_COL, SLOTS, BLOCK, BLOCK, C))

    crop_grad32 = crop_grad.reshape(N_STRIP, N_COL, SLOTS, BLOCK, BLOCK, C).astype(jnp.float32)
    column_pass = jnp.einsum("ncskx,ncsikh->ncsixh", col_weight, crop_grad32, precision=lax.Precision.HIGHEST)
    tile_grads = jnp.einsum("ncsiy,ncsixh->ncyxh", row_weight, column_pass, precision=lax.Precision.HIGHEST)
    grad_features = tile_grads.transpose(0, 2, 1, 3, 4).reshape(N_STRIP * ROWS, N_COL * COLS, C).astype(jnp.bfloat16)
    return mask_features, grad_features
```

```python
import functools

import jax
import jax.numpy as jnp
from jax import lax
from jax.experimental import pallas as pl
from jax.experimental.pallas import tpu as pltpu
from jax.sharding import PartitionSpec as P

MESH = pl.DeviceIdType.MESH
VMEM_BYTES = 56 * 1024 * 1024
EDGE = 16
OFFSETS = [(dy, dx, dc) for dy in (0, -1, 1) for dx in (0, -1, 1) for dc in (1, 0) if (dy, dx, dc) != (0, 0, 0)]


def spread_kernel(strips, cols, f_ref, w0, w1, w2, w3, pad_ref, o0, o1, o2, o3, send_sem, recv_sem, own_sem):
    strip, col, chan = (lax.axis_index("strip"), lax.axis_index("col"), lax.axis_index("chan"))
    rows, width, half = f_ref.shape
    lanes = pl.ds(pl.multiple_of(chan * half, half), half)

    def there(dy, dx):
        return (strip + dy >= 0) & (strip + dy < strips) & (col + dx >= 0) & (col + dx < cols)

    def target(dy, dx, dc):
        return {"strip": strip + dy, "col": col + dx, "chan": (chan + dc) % 2}

    barrier = pltpu.get_barrier_semaphore()
    for dy, dx, dc in OFFSETS:

        @pl.when(there(dy, dx))
        def _():
            pl.semaphore_signal(barrier, inc=1, device_id=target(dy, dx, dc), device_id_type=MESH)

    near_rows = 1 + jnp.where(strip > 0, 1, 0) + jnp.where(strip < strips - 1, 1, 0)
    near_cols = 1 + jnp.where(col > 0, 1, 0) + jnp.where(col < cols - 1, 1, 0)
    pl.semaphore_wait(barrier, 2 * near_rows * near_cols - 1)

    row_from = {0: (0, rows), 1: (rows - 2, 2), -1: (0, 2)}
    row_to = {0: 2, 1: 0, -1: rows + 2}
    col_from = {0: (0, width), 1: (width - EDGE, EDGE), -1: (0, EDGE)}
    col_to = {0: EDGE, 1: 0, -1: width + EDGE}

    def halo(at):
        dy, dx, dc = OFFSETS[at]
        row, row_count = row_from[dy]
        first, count = col_from[dx]
        return pltpu.make_async_remote_copy(
            src_ref=f_ref.at[pl.ds(row, row_count), pl.ds(first, count)],
            dst_ref=pad_ref.at[pl.ds(row_to[dy], row_count), pl.ds(col_to[dx], count), lanes],
            send_sem=send_sem.at[at],
            recv_sem=recv_sem.at[at],
            device_id=target(dy, dx, dc),
            device_id_type=MESH,
        )

    count = len(OFFSETS)
    pairs = ((w0, o0), (w1, o1), (w2, o2), (w3, o3))
    weights = [
        pltpu.make_async_remote_copy(
            src_ref=w,
            dst_ref=o.at[:, :, lanes],
            send_sem=send_sem.at[count + i],
            recv_sem=recv_sem.at[count + i],
            device_id=target(0, 0, 1),
            device_id_type=MESH,
        )
        for i, (w, o) in enumerate(pairs)
    ]
    for at, (dy, dx, dc) in enumerate(OFFSETS):

        @pl.when(there(dy, dx))
        def _():
            halo(at).start()

    for copy in weights:
        copy.start()
    own = [pltpu.make_async_copy(w, o.at[:, :, lanes], own_sem.at[i]) for i, (w, o) in enumerate(pairs)]
    own.append(
        pltpu.make_async_copy(f_ref, pad_ref.at[pl.ds(2, rows), pl.ds(EDGE, width), lanes], own_sem.at[4])
    )
    for copy in own:
        copy.start()
    for copy in own:
        copy.wait()
    for at, (dy, dx, dc) in enumerate(OFFSETS):

        @pl.when(there(dy, dx))
        def _():
            halo(at).wait_send()

        @pl.when(there(-dy, -dx))
        def _():
            halo(at).wait_recv()

    for copy in weights:
        copy.wait()


def spread(features, weights, strips, cols):
    rows, width, half = features.shape
    full = [jax.ShapeDtypeStruct(w.shape[:2] + (2 * half,), w.dtype) for w in weights]
    count = len(OFFSETS) + 4
    any_spec = pl.BlockSpec(memory_space=pl.ANY)
    return pl.pallas_call(
        functools.partial(spread_kernel, strips, cols),
        out_shape=[jax.ShapeDtypeStruct((rows + 4, width + 2 * EDGE, 2 * half), features.dtype)] + full,
        in_specs=[any_spec] * 5,
        out_specs=[any_spec] * 5,
        scratch_shapes=[
            pltpu.SemaphoreType.DMA((count,)),
            pltpu.SemaphoreType.DMA((count,)),
            pltpu.SemaphoreType.DMA((5,)),
        ],
        compiler_params=pltpu.CompilerParams(collective_id=0, has_side_effects=True),
        name="spread",
    )(features, *weights)


def sigmoid(v):
    return 1.0 / (1.0 + jnp.exp(-v))


def taps(v):
    count = v.shape[0]
    return (pltpu.roll(v, 1, 0), v, pltpu.roll(v, count - 1, 0))


def dot(a, b):
    return jnp.dot(a, b, preferred_element_type=jnp.float32)


def dot_t(a, b):
    return lax.dot_general(a, b, (((1,), (1,)), ((), ())), preferred_element_type=jnp.float32)


def sample_weight(start, length, index, cell, samples):
    twice = 2 * samples
    num = twice * start + (2 * index + 1) * length - samples
    last = start + length - 1
    num = jnp.minimum(jnp.maximum(num, twice * start), twice * last)
    low = (num * 2341) >> 16
    frac = (num - twice * low).astype(jnp.float32) / twice
    high = jnp.minimum(low + 1, last)
    return jnp.where(cell == low, 1.0 - frac, 0.0) + jnp.where(cell == high, frac, 0.0)


def forward_kernel(
    samples, group, meta, pad_ref, t1, t2, m1, m2, send_ref, slope1_ref, slope2_ref, s0, s1, feat, sc, sa
):
    prows, pwidth, chans = pad_ref.shape
    rows, width = (prows - 4, pwidth - 2 * EDGE)
    regions = slope1_ref.shape[0]
    half = chans // 2
    info = 6 * regions
    strip, strips, col, cols = (meta[info], meta[info + 1], meta[info + 2], meta[info + 3])
    top_ok, bottom_ok = (strip > 0, strip < strips - 1)

    x_ids = lax.broadcasted_iota(jnp.int32, (pwidth, 1), 0)
    x_lo = jnp.where(col > 0, 0, EDGE)
    x_hi = jnp.where(col < cols - 1, pwidth, EDGE + width)
    x_ok = (x_ids >= x_lo) & (x_ids < x_hi)

    def fill_row(y, carry):
        y_lo = jnp.where(top_ok, 0, 2)
        y_hi = jnp.where(bottom_ok, prows, prows - 2)
        ok = x_ok & (y >= y_lo) & (y < y_hi)
        v = jnp.where(ok, pad_ref[y].astype(jnp.float32), 0.0)
        for b, t in enumerate(taps(v)):
            s0[pl.ds(y * pwidth, pwidth), b * chans : (b + 1) * chans] = t.astype(jnp.bfloat16)
        return carry

    lax.fori_loop(0, prows, fill_row, 0, unroll=4)

    hid_rows = prows - 2
    step = 6
    size = step * pwidth
    ids = lax.broadcasted_iota(jnp.int32, (size, 1), 0)
    sub_row = ids // pwidth
    sub_col = ids % pwidth

    def hidden_chunk(i, carry):
        acc = None
        for a in range(3):
            term = dot(s0[pl.ds(pl.multiple_of((i * step + a) * pwidth, pwidth), size), :], t1[a])
            acc = term if acc is None else acc + term
        y = sub_row + i * step
        y_lo = jnp.where(top_ok, 0, 1)
        y_hi = jnp.where(bottom_ok, hid_rows, hid_rows - 1)
        ok = (sub_col >= x_lo) & (sub_col < x_hi) & (y >= y_lo) & (y < y_hi)
        v = jnp.where(ok, acc * sigmoid(acc), 0.0)
        for b, t in enumerate(taps(v)):
            s1[pl.ds(pl.multiple_of(i * size, size), size), b * chans : (b + 1) * chans] = t.astype(jnp.bfloat16)
        return carry

    lax.fori_loop(0, hid_rows // step, hidden_chunk, 0)

    fstep = 8
    fsize = fstep * pwidth

    def feat_chunk(i, carry):
        acc = None
        for a in range(3):
            term = dot(s1[pl.ds(pl.multiple_of((i * fstep + a) * pwidth, pwidth), fsize), :], t2[a])
            acc = term if acc is None else acc + term
        v = (acc * sigmoid(acc)).reshape(fstep, pwidth, chans)[:, EDGE : EDGE + width, :]
        feat[pl.ds(pl.multiple_of(i * fstep * width, fstep * width), fstep * width), :] = v.reshape(
            fstep * width, chans
        ).astype(jnp.bfloat16)
        return carry

    lax.fori_loop(0, rows // fstep, feat_chunk, 0)

    block = samples * EDGE
    p = lax.broadcasted_iota(jnp.int32, (block, 1), 0)
    i_id, k_id = (p // EDGE, p % EDGE)
    q = lax.broadcasted_iota(jnp.int32, (1, rows * width), 1)
    y_id, x_id = (q // width, q % width)
    live = k_id < samples
    zeros = jnp.zeros((EDGE, 3 * chans), jnp.bfloat16)

    def put(dst, r, v):
        for b, t in enumerate(taps(v)):
            dst[r, EDGE : EDGE + block, b * chans : (b + 1) * chans] = t.astype(jnp.bfloat16)

    def crop_one(r, carry):
        row = sample_weight(meta[4 * r], meta[4 * r + 2], i_id, y_id, samples)
        column = sample_weight(meta[4 * r + 1], meta[4 * r + 3], k_id, x_id, samples)
        weight = jnp.where(live, row * column, 0.0).astype(jnp.bfloat16)
        put(sc, r, dot(weight, feat[...]))
        for dst in (sc, sa):
            dst[r, 0:EDGE, :] = zeros
            dst[r, EDGE + block : 2 * EDGE + block, :] = zeros
        return carry

    lax.fori_loop(0, regions, crop_one, 0)

    def conv(src, g, w):
        acc = None
        for a in range(3):
            lhs = src[pl.ds(g * group, group), a * EDGE : a * EDGE + block, :].reshape(group * block, 3 * chans)
            term = dot(lhs, w[a])
            acc = term if acc is None else acc + term
        return acc.reshape(group, block, chans)

    def first_layer(g, carry):
        pre = conv(sc, g, m1)
        for n in range(group):
            v = pre[n]
            s = sigmoid(v)
            slope1_ref[g * group + n] = s * (1.0 + v * (1.0 - s))
            put(sa, g * group + n, jnp.where(live, v * s, 0.0))
        return carry

    lax.fori_loop(0, regions // group, first_layer, 0)

    def second_layer(g, carry):
        pre = conv(sa, g, m2)
        for n in range(group):
            r = g * group + n
            v = pre[n]
            s = sigmoid(v)
            slope2_ref[r] = s * (1.0 + v * (1.0 - s))
            out = (v * s).astype(jnp.bfloat16)
            owner, place = (meta[4 * regions + r], meta[5 * regions + r])
            send_ref[2 * owner, place] = out[:, :half]
            send_ref[2 * owner + 1, place] = out[:, half:]
        return carry

    lax.fori_loop(0, regions // group, second_layer, 0)


def backward_kernel(samples, group, meta, cot_ref, slope1_ref, slope2_ref, m1, m2, grad_ref, sg, mt, cg):
    regions, block, chans = slope1_ref.shape
    half = chans // 2
    rows, width = grad_ref.shape[1], grad_ref.shape[2]
    k_id = lax.broadcasted_iota(jnp.int32, (block, 1), 0) % EDGE
    live = k_id < samples
    zeros = jnp.zeros((EDGE, 3 * chans), jnp.bfloat16)
    q = lax.broadcasted_iota(jnp.int32, (rows * width, 1), 0)
    y_id, x_id = (q // width, q % width)
    p = lax.broadcasted_iota(jnp.int32, (1, block), 1)
    i_id, kk_id = (p // EDGE, p % EDGE)

    def put(r, v):
        for b, t in enumerate(taps(v)):
            sg[r, EDGE : EDGE + block, b * chans : (b + 1) * chans] = t.astype(jnp.bfloat16)

    def start(r, carry):
        sg[r, 0:EDGE, :] = zeros
        sg[r, EDGE + block : 2 * EDGE + block, :] = zeros
        owner, place = (meta[4 * regions + r], meta[5 * regions + r])
        for c in range(2):
            lanes = slice(c * half, (c + 1) * half)
            cot = cot_ref[2 * owner + c, place].astype(jnp.float32)
            grad = jnp.where(live, cot * slope2_ref[r, :, lanes], 0.0)
            for b, t in enumerate(taps(grad)):
                at = b * chans + c * half
                sg[r, EDGE : EDGE + block, at : at + half] = t.astype(jnp.bfloat16)
        row = sample_weight(meta[4 * r], meta[4 * r + 2], i_id, y_id, samples)
        column = sample_weight(meta[4 * r + 1], meta[4 * r + 3], kk_id, x_id, samples)
        mt[r] = jnp.where(kk_id < samples, row * column, 0.0).astype(jnp.bfloat16)
        return carry

    lax.fori_loop(0, regions, start, 0)

    def back(g, w):
        acc = None
        for a in range(3):
            for b in range(3):
                lhs = sg[
                    pl.ds(g * group, group), a * EDGE : a * EDGE + block, b * chans : (b + 1) * chans
                ].reshape(group * block, chans)
                term = dot_t(lhs, w[2 - a, (2 - b) * chans : (3 - b) * chans, :])
                acc = term if acc is None else acc + term
        return acc.reshape(group, block, chans)

    def second(g, carry):
        d = back(g, m2)
        for n in range(group):
            r = g * group + n
            put(r, jnp.where(live, d[n] * slope1_ref[r], 0.0))
        return carry

    lax.fori_loop(0, regions // group, second, 0)

    def first(g, carry):
        d = back(g, m1)
        for n in range(group):
            cg[g * group + n] = d[n].astype(jnp.bfloat16)
        return carry

    lax.fori_loop(0, regions // group, first, 0)

    total = None
    for r in range(regions):
        term = dot(mt[r], cg[r])
        total = term if total is None else total + term
    for c in range(2):
        grad_ref[c] = total[:, c * half : (c + 1) * half].reshape(rows, width, half)


def place_kernel(capacity, source, live, got_ref, out_ref):
    samples = out_ref.shape[1]

    def one(n, carry):
        block = got_ref[source[n]].reshape(samples, EDGE, -1)[:, :samples, :]
        out_ref[n] = jnp.where(live[n] > 0, block, jnp.zeros_like(block))
        return carry

    lax.fori_loop(0, capacity, one, 0)


def shards(
    features, tile_first, tile_second, mask_first, mask_second, region_boxes, owner_strip, cotangent
):
    rows, width, half = features.shape
    chans = 2 * half
    capacity, samples = (cotangent.shape[2], cotangent.shape[3])
    block = samples * EDGE
    strips, cols = (lax.axis_size("strip"), lax.axis_size("col"))
    strip_at, col_at, chan_at = (lax.axis_index("strip"), lax.axis_index("col"), lax.axis_index("chan"))
    slots = owner_strip.shape[2]
    regions = slots // 2
    per_pair = -(-capacity // strips)
    per_core = -(-per_pair // 2)
    vmem = pl.BlockSpec(memory_space=pltpu.VMEM)
    smem = pl.BlockSpec(memory_space=pltpu.SMEM)

    all_owners = lax.all_gather(owner_strip, "strip", axis=0, tiled=True)[:, 0, :]
    mine = (all_owners == strip_at).astype(jnp.int32)
    number = (jnp.cumsum(mine.reshape(-1)) - 1).reshape(strips, regions, 2)
    mine = mine.reshape(strips, regions, 2)
    place = jnp.cumsum(mine, axis=1) - 1
    chosen = (
        (mine[..., None, None] > 0)
        & (place[..., None, None] == jnp.arange(per_core, dtype=jnp.int32)[:, None])
        & (number[..., None, None] == jnp.arange(capacity, dtype=jnp.int32))
    )
    select = jnp.any(chosen, axis=1).reshape(strips * 2 * per_core, capacity)
    source = jnp.sum(
        jnp.where(select, jnp.arange(strips * 2 * per_core, dtype=jnp.int32)[:, None], 0), axis=0
    ).astype(jnp.int32)
    used = jnp.any(select, axis=0).astype(jnp.int32)
    sent = jnp.einsum(
        "dm,mikh->dikh", select.astype(jnp.bfloat16), cotangent[0, 0], preferred_element_type=jnp.float32
    ).astype(jnp.bfloat16)
    sent = jnp.pad(sent, ((0, 0), (0, 0), (0, EDGE - samples), (0, 0))).reshape(
        2 * strips, per_core, block, half
    )
    cots = lax.all_to_all(sent, ("strip", "chan"), split_axis=0, concat_axis=0, tiled=True)

    my_owners = lax.dynamic_index_in_dim(owner_strip[0, 0].reshape(regions, 2), chan_at, 1, False)
    my_boxes = lax.dynamic_index_in_dim(region_boxes[0, 0].reshape(regions, 2, 4), chan_at, 1, False)
    ids = jnp.arange(regions, dtype=jnp.int32)
    rank = jnp.sum(
        ((my_owners[:, None] == my_owners[None, :]) & (ids[None, :] < ids[:, None])).astype(jnp.int32), axis=1
    )
    base = jnp.stack([strip_at * rows, col_at * width, jnp.int32(0), jnp.int32(0)]).astype(jnp.int32)
    meta = jnp.concatenate(
        [
            (my_boxes - base).reshape(-1),
            my_owners,
            rank.astype(jnp.int32),
            jnp.stack([strip_at, jnp.int32(strips), col_at, jnp.int32(cols)]).astype(jnp.int32),
        ]
    )

    weights = [w.reshape(3, 3 * chans, half) for w in (tile_first, tile_second, mask_first, mask_second)]
    padded, t1, t2, m1, m2 = spread(features, weights, strips, cols)

    group = 2
    prows, pwidth = (rows + 4, width + 2 * EDGE)
    masks, slope1, slope2 = pl.pallas_call(
        functools.partial(forward_kernel, samples, group),
        out_shape=[
            jax.ShapeDtypeStruct((2 * strips, per_core, block, half), jnp.bfloat16),
            jax.ShapeDtypeStruct((regions, block, chans), jnp.float32),
            jax.ShapeDtypeStruct((regions, block, chans), jnp.float32),
        ],
        in_specs=[smem] + [vmem] * 5,
        out_specs=[vmem] * 3,
        scratch_shapes=[
            pltpu.VMEM((prows * pwidth, 3 * chans), jnp.bfloat16),
            pltpu.VMEM(((prows - 2) * pwidth, 3 * chans), jnp.bfloat16),
            pltpu.VMEM((rows * width, chans), jnp.bfloat16),
            pltpu.VMEM((regions, block + 2 * EDGE, 3 * chans), jnp.bfloat16),
            pltpu.VMEM((regions, block + 2 * EDGE, 3 * chans), jnp.bfloat16),
        ],
        compiler_params=pltpu.CompilerParams(vmem_limit_bytes=VMEM_BYTES),
        cost_estimate=pl.CostEstimate(flops=12 * 10**9, bytes_accessed=10**7, transcendentals=0),
        name="forward",
    )(meta, padded, t1, t2, m1, m2)

    got = lax.all_to_all(masks, ("strip", "chan"), split_axis=0, concat_axis=0, tiled=True)

    grads = pl.pallas_call(
        functools.partial(backward_kernel, samples, group),
        out_shape=jax.ShapeDtypeStruct((2, rows, width, half), jnp.float32),
        in_specs=[smem] + [vmem] * 5,
        out_specs=vmem,
        scratch_shapes=[
            pltpu.VMEM((regions, block + 2 * EDGE, 3 * chans), jnp.bfloat16),
            pltpu.VMEM((regions, rows * width, block), jnp.bfloat16),
            pltpu.VMEM((regions, block, chans), jnp.bfloat16),
        ],
        compiler_params=pltpu.CompilerParams(vmem_limit_bytes=VMEM_BYTES),
        cost_estimate=pl.CostEstimate(flops=12 * 10**9, bytes_accessed=10**7, transcendentals=0),
        name="backward",
    )(meta, cots, slope1, slope2, m1, m2)

    other = lax.ppermute(
        lax.dynamic_index_in_dim(grads, 1 - chan_at, 0, False), "chan", [(0, 1), (1, 0)]
    )
    grad_tile = (lax.dynamic_index_in_dim(grads, chan_at, 0, False) + other).astype(jnp.bfloat16)

    mask_out = pl.pallas_call(
        functools.partial(place_kernel, capacity),
        out_shape=jax.ShapeDtypeStruct((capacity, samples, samples, half), jnp.bfloat16),
        in_specs=[smem, smem, vmem],
        out_specs=vmem,
        compiler_params=pltpu.CompilerParams(vmem_limit_bytes=VMEM_BYTES),
        name="place",
    )(source, used, got.reshape(2 * strips * per_core, block, half))
    return (mask_out[None, None], grad_tile)


def solution(mesh):
    placed = (
        P(("grp", "strip"), "col", "chan"),
        P(None, None, None, "chan"),
        P(None, None, None, "chan"),
        P(None, None, None, "chan"),
        P(None, None, None, "chan"),
        P(("grp", "strip"), "col", None, None),
        P(("grp", "strip"), "col", None),
        P(("grp", "strip"), "col", None, None, None, "chan"),
    )
    return jax.shard_map(
        shards,
        mesh=mesh,
        in_specs=placed,
        out_specs=(
            P(("grp", "strip"), "col", None, None, None, "chan"),
            P(("grp", "strip"), "col", "chan"),
        ),
        check_vma=False,
    )
```

```python
import functools

import jax
import jax.numpy as jnp
from jax import lax
from jax.experimental import pallas as pl
from jax.experimental.pallas import tpu as pltpu
from jax.sharding import PartitionSpec as P

MESH = pl.DeviceIdType.MESH
VMEM_BYTES = 56 * 1024 * 1024
EDGE = 16
OFFSETS = [(dy, dx, dc) for dy in (0, -1, 1) for dx in (0, -1, 1) for dc in (1, 0) if (dy, dx, dc) != (0, 0, 0)]


def sigmoid(v):
    return 1.0 / (1.0 + jnp.exp(-v))


def taps(v):
    count = v.shape[0]
    return (pltpu.roll(v, 1, 0), v, pltpu.roll(v, count - 1, 0))


def dot(a, b):
    return jnp.dot(a, b, preferred_element_type=jnp.float32)


def dot_t(a, b):
    return lax.dot_general(a, b, (((1,), (1,)), ((), ())), preferred_element_type=jnp.float32)


def both(w, a, rows=slice(None)):
    return jnp.concatenate([w[0, a, rows, :], w[1, a, rows, :]], axis=-1)


def sample_weight(start, length, index, cell, samples):
    twice = 2 * samples
    num = twice * start + (2 * index + 1) * length - samples
    last = start + length - 1
    num = jnp.minimum(jnp.maximum(num, twice * start), twice * last)
    low = (num * 2341) >> 16
    frac = (num - twice * low).astype(jnp.float32) / twice
    high = jnp.minimum(low + 1, last)
    return jnp.where(cell == low, 1.0 - frac, 0.0) + jnp.where(cell == high, frac, 0.0)


def head_kernel(
    strips,
    cols,
    group,
    boxes,
    owners,
    owner_row,
    f_ref,
    w0,
    w1,
    w2,
    w3,
    cot_in,
    mask_ref,
    grad_ref,
    pad_ref,
    t1,
    t2,
    m1,
    m2,
    own_tile,
    all_tile,
    all_owner,
    table,
    cot_out,
    cot_got,
    mask_out,
    mask_got,
    part,
    part_got,
    s0,
    s1,
    feat,
    sc,
    sa,
    slope1,
    slope2,
    mask_own,
    mt,
    cg,
    halo_send,
    halo_recv,
    weight_send,
    weight_recv,
    owner_send,
    owner_recv,
    cot_send,
    cot_recv,
    mask_send,
    mask_recv,
    part_sem,
    own_sem,
):
    strip, col, chan = (lax.axis_index("strip"), lax.axis_index("col"), lax.axis_index("chan"))
    rows, width, half = f_ref.shape
    chans = 2 * half
    capacity, samples = (mask_ref.shape[0], mask_ref.shape[1])
    regions = slope1.shape[0]
    per_core = cot_out.shape[1]
    prows, pwidth = (pad_ref.shape[1], pad_ref.shape[2])
    block = samples * EDGE
    peers = 2 * strips
    me = strip * 2 + chan

    def there(dy, dx):
        return (strip + dy >= 0) & (strip + dy < strips) & (col + dx >= 0) & (col + dx < cols)

    def near(dy, dx, dc):
        return {"strip": strip + dy, "col": col + dx, "chan": (chan + dc) % 2}

    def peer(d):
        other = lax.rem(me + d, peers)
        return {"strip": other // 2, "chan": lax.rem(other, 2)}

    barrier = pltpu.get_barrier_semaphore()
    for dy, dx, dc in OFFSETS:
        if dx != 0:

            @pl.when(there(dy, dx))
            def _():
                pl.semaphore_signal(barrier, inc=1, device_id=near(dy, dx, dc), device_id_type=MESH)

    def greet(d, carry):
        pl.semaphore_signal(barrier, inc=1, device_id=peer(d), device_id_type=MESH)
        return carry

    lax.fori_loop(1, peers, greet, 0)
    near_rows = 1 + jnp.where(strip > 0, 1, 0) + jnp.where(strip < strips - 1, 1, 0)
    near_cols = jnp.where(col > 0, 1, 0) + jnp.where(col < cols - 1, 1, 0)
    own_tile[...] = jnp.zeros_like(own_tile)
    own_tile[0:1, 0 : owner_row.shape[1]] = owner_row[...]
    pl.semaphore_wait(barrier, 2 * near_rows * near_cols + peers - 1)

    def owner_copy(d):
        return pltpu.make_async_remote_copy(
            src_ref=own_tile,
            dst_ref=all_tile.at[strip],
            send_sem=owner_send.at[d],
            recv_sem=owner_recv.at[d],
            device_id={"strip": lax.rem(strip + d, strips)},
            device_id_type=MESH,
        )

    def start_owner(d, carry):
        owner_copy(d).start()
        return carry

    lax.fori_loop(1, strips, start_owner, 0)

    row_from = {0: (0, rows), 1: (rows - 2, 2), -1: (0, 2)}
    row_to = {0: 2, 1: 0, -1: rows + 2}
    col_from = {0: (0, width), 1: (width - EDGE, EDGE), -1: (0, EDGE)}
    col_to = {0: EDGE, 1: 0, -1: width + EDGE}

    def halo(at):
        dy, dx, dc = OFFSETS[at]
        row, row_count = row_from[dy]
        first, count = col_from[dx]
        return pltpu.make_async_remote_copy(
            src_ref=f_ref.at[pl.ds(row, row_count), pl.ds(first, count)],
            dst_ref=pad_ref.at[chan, pl.ds(row_to[dy], row_count), pl.ds(col_to[dx], count)],
            send_sem=halo_send.at[at],
            recv_sem=halo_recv.at[at],
            device_id=near(dy, dx, dc),
            device_id_type=MESH,
        )

    pairs = ((w0, t1), (w1, t2), (w2, m1), (w3, m2))
    weights = [
        pltpu.make_async_remote_copy(
            src_ref=w,
            dst_ref=o.at[chan],
            send_sem=weight_send.at[i],
            recv_sem=weight_recv.at[i],
            device_id=near(0, 0, 1),
            device_id_type=MESH,
        )
        for i, (w, o) in enumerate(pairs)
    ]
    for at, (dy, dx, dc) in enumerate(OFFSETS):

        @pl.when(there(dy, dx))
        def _():
            halo(at).start()

    for copy in weights:
        copy.start()
    own = [pltpu.make_async_copy(w, o.at[chan], own_sem.at[i]) for i, (w, o) in enumerate(pairs)]
    own.append(
        pltpu.make_async_copy(f_ref, pad_ref.at[chan, pl.ds(2, rows), pl.ds(EDGE, width)], own_sem.at[4])
    )
    for copy in own:
        copy.start()

    all_tile[strip] = own_tile[...]

    def clear(i, carry):
        cot_out[i] = jnp.zeros(cot_out.shape[1:], cot_out.dtype)
        return carry

    lax.fori_loop(0, peers, clear, 0)

    def wait_owner(d, carry):
        owner_copy(d).wait()
        return carry

    lax.fori_loop(1, strips, wait_owner, 0)
    to_scalar = pltpu.make_async_copy(all_tile, all_owner, own_sem.at[5])
    to_scalar.start()
    to_scalar.wait()

    def find(s, number):
        for core in range(2):
            for p in range(per_core):
                table[(2 * s + core) * per_core + p] = jnp.int32(-1)
        seen = [jnp.int32(0), jnp.int32(0)]
        held = [[jnp.int32(-1)] * per_core, [jnp.int32(-1)] * per_core]
        for at in range(2 * regions):
            core = at % 2
            hit = all_owner[s, 0, at] == strip
            for p in range(per_core):
                held[core][p] = jnp.where(hit & (seen[core] == p), number, held[core][p])
            one = jnp.where(hit, 1, 0)
            seen[core] = seen[core] + one
            number = number + one
        for core in range(2):
            for p in range(per_core):
                table[(2 * s + core) * per_core + p] = held[core][p]
        return number

    lax.fori_loop(0, strips, find, jnp.int32(0))

    def choose(i, carry):
        for p in range(per_core):
            slot = jnp.clip(table[i * per_core + p], 0, capacity - 1)
            cot_out[i, p, :, 0:samples, :] = cot_in[slot]
        return carry

    lax.fori_loop(0, peers, choose, 0)

    def block_copy(src, dst, send, recv, d):
        return pltpu.make_async_remote_copy(
            src_ref=src.at[lax.rem(me + d, peers)],
            dst_ref=dst.at[me],
            send_sem=send.at[d],
            recv_sem=recv.at[d],
            device_id=peer(d),
            device_id_type=MESH,
        )

    def start_cot(d, carry):
        block_copy(cot_out, cot_got, cot_send, cot_recv, d).start()
        return carry

    lax.fori_loop(1, peers, start_cot, 0)
    cot_got[me] = cot_out[me]

    for copy in own:
        copy.wait()
    for at, (dy, dx, dc) in enumerate(OFFSETS):

        @pl.when(there(-dy, -dx))
        def _():
            halo(at).wait_recv()

    weights[0].wait_recv()
    top_ok, bottom_ok = (strip > 0, strip < strips - 1)
    x_ids = lax.broadcasted_iota(jnp.int32, (pwidth, 1), 0)
    x_lo = jnp.where(col > 0, 0, EDGE)
    x_hi = jnp.where(col < cols - 1, pwidth, EDGE + width)
    x_ok = (x_ids >= x_lo) & (x_ids < x_hi)

    def fill_row(y, carry):
        y_lo = jnp.where(top_ok, 0, 2)
        y_hi = jnp.where(bottom_ok, prows, prows - 2)
        ok = x_ok & (y >= y_lo) & (y < y_hi)
        for c in range(2):
            v = jnp.where(ok, pad_ref[c, y].astype(jnp.float32), 0.0)
            for b, t in enumerate(taps(v)):
                at = b * chans + c * half
                s0[pl.ds(y * pwidth, pwidth), at : at + half] = t.astype(jnp.bfloat16)
        return carry

    lax.fori_loop(0, prows, fill_row, 0, unroll=4)

    hid_rows = prows - 2
    step = 6
    size = step * pwidth
    ids = lax.broadcasted_iota(jnp.int32, (size, 1), 0)
    sub_row = ids // pwidth
    sub_col = ids % pwidth

    def hidden_chunk(i, carry):
        acc = None
        for a in range(3):
            term = dot(s0[pl.ds(pl.multiple_of((i * step + a) * pwidth, pwidth), size), :], both(t1, a))
            acc = term if acc is None else acc + term
        y = sub_row + i * step
        y_lo = jnp.where(top_ok, 0, 1)
        y_hi = jnp.where(bottom_ok, hid_rows, hid_rows - 1)
        ok = (sub_col >= x_lo) & (sub_col < x_hi) & (y >= y_lo) & (y < y_hi)
        v = jnp.where(ok, acc * sigmoid(acc), 0.0)
        for b, t in enumerate(taps(v)):
            s1[pl.ds(pl.multiple_of(i * size, size), size), b * chans : (b + 1) * chans] = t.astype(jnp.bfloat16)
        return carry

    lax.fori_loop(0, hid_rows // step, hidden_chunk, 0)

    weights[1].wait_recv()
    fstep = 8
    fsize = fstep * pwidth

    def feat_chunk(i, carry):
        acc = None
        for a in range(3):
            term = dot(s1[pl.ds(pl.multiple_of((i * fstep + a) * pwidth, pwidth), fsize), :], both(t2, a))
            acc = term if acc is None else acc + term
        v = (acc * sigmoid(acc)).reshape(fstep, pwidth, chans)[:, EDGE : EDGE + width, :]
        feat[pl.ds(pl.multiple_of(i * fstep * width, fstep * width), fstep * width), :] = v.reshape(
            fstep * width, chans
        ).astype(jnp.bfloat16)
        return carry

    lax.fori_loop(0, rows // fstep, feat_chunk, 0)

    block = samples * EDGE
    p = lax.broadcasted_iota(jnp.int32, (block, 1), 0)
    i_id, k_id = (p // EDGE, p % EDGE)
    q = lax.broadcasted_iota(jnp.int32, (1, rows * width), 1)
    y_id, x_id = (q // width, q % width)
    live = k_id < samples
    zeros = jnp.zeros((EDGE, 3 * chans), jnp.bfloat16)

    def put(dst, r, v):
        for b, t in enumerate(taps(v)):
            dst[r, EDGE : EDGE + block, b * chans : (b + 1) * chans] = t.astype(jnp.bfloat16)

    def crop_one(r, carry):
        row = sample_weight(boxes[2 * r + chan, 0] - strip * rows, boxes[2 * r + chan, 2], i_id, y_id, samples)
        column = sample_weight(boxes[2 * r + chan, 1] - col * width, boxes[2 * r + chan, 3], k_id, x_id, samples)
        weight = jnp.where(live, row * column, 0.0).astype(jnp.bfloat16)
        put(sc, r, dot(weight, feat[...]))
        for dst in (sc, sa):
            dst[r, 0:EDGE, :] = zeros
            dst[r, EDGE + block : 2 * EDGE + block, :] = zeros
        return carry

    lax.fori_loop(0, regions, crop_one, 0)

    def conv(src, g, w):
        acc = None
        for a in range(3):
            lhs = src[pl.ds(g * group, group), a * EDGE : a * EDGE + block, :].reshape(group * block, 3 * chans)
            term = dot(lhs, both(w, a))
            acc = term if acc is None else acc + term
        return acc.reshape(group, block, chans)

    weights[2].wait_recv()

    def first_layer(g, carry):
        pre = conv(sc, g, m1)
        for n in range(group):
            v = pre[n]
            s = sigmoid(v)
            slope1[g * group + n] = s * (1.0 + v * (1.0 - s))
            put(sa, g * group + n, jnp.where(live, v * s, 0.0))
        return carry

    lax.fori_loop(0, regions // group, first_layer, 0)

    weights[3].wait_recv()

    def second_layer(g, carry):
        pre = conv(sa, g, m2)
        for n in range(group):
            r = g * group + n
            v = pre[n]
            s = sigmoid(v)
            slope2[r] = s * (1.0 + v * (1.0 - s))
            mask_own[r] = (v * s).astype(jnp.bfloat16)
        return carry

    lax.fori_loop(0, regions // group, second_layer, 0)

    mine = [owners[2 * r + chan] for r in range(regions)]
    rank = []
    for r in range(regions):
        total = jnp.int32(0)
        for before in range(r):
            total = total + jnp.where(mine[before] == mine[r], 1, 0)
        rank.append(total)

    def gather_mask(o, carry):
        for p in range(per_core):
            pick = jnp.int32(0)
            for r in range(regions):
                pick = jnp.where((mine[r] == o) & (rank[r] == p), r, pick)
            out = mask_own[pick]
            for c in range(2):
                mask_out[2 * o + c, p] = out[:, c * half : (c + 1) * half].reshape(samples, EDGE, half)
        return carry

    lax.fori_loop(0, strips, gather_mask, 0)

    def start_mask(d, carry):
        block_copy(mask_out, mask_got, mask_send, mask_recv, d).start()
        return carry

    lax.fori_loop(1, peers, start_mask, 0)
    mask_got[me] = mask_out[me]

    def wait_cot(d, carry):
        block_copy(cot_out, cot_got, cot_send, cot_recv, d).wait()
        return carry

    lax.fori_loop(1, peers, wait_cot, 0)

    yt = lax.broadcasted_iota(jnp.int32, (rows * width, 1), 0)
    yt_id, xt_id = (yt // width, yt % width)
    pt = lax.broadcasted_iota(jnp.int32, (1, block), 1)
    it_id, kt_id = (pt // EDGE, pt % EDGE)

    def start_grad(r, carry):
        place = jnp.int32(0)
        owner = owners[2 * r + chan]
        for before in range(regions):
            same = (mine[before] == owner) & (before < r)
            place = place + jnp.where(same, 1, 0)
        place = jnp.minimum(place, per_core - 1)
        for c in range(2):
            lanes = slice(c * half, (c + 1) * half)
            cot = cot_got[2 * owner + c, place].reshape(block, half).astype(jnp.float32)
            grad = jnp.where(live, cot * slope2[r, :, lanes], 0.0)
            for b, t in enumerate(taps(grad)):
                at = b * chans + c * half
                sc[r, EDGE : EDGE + block, at : at + half] = t.astype(jnp.bfloat16)
        row = sample_weight(
            boxes[2 * r + chan, 0] - strip * rows, boxes[2 * r + chan, 2], it_id, yt_id, samples
        )
        column = sample_weight(
            boxes[2 * r + chan, 1] - col * width, boxes[2 * r + chan, 3], kt_id, xt_id, samples
        )
        mt[r] = jnp.where(kt_id < samples, row * column, 0.0).astype(jnp.bfloat16)
        return carry

    lax.fori_loop(0, regions, start_grad, 0)

    def back(src, g, w):
        acc = None
        for a in range(3):
            for b in range(3):
                lhs = src[
                    pl.ds(g * group, group), a * EDGE : a * EDGE + block, b * chans : (b + 1) * chans
                ].reshape(group * block, chans)
                term = dot_t(lhs, both(w, 2 - a, slice((2 - b) * chans, (3 - b) * chans)))
                acc = term if acc is None else acc + term
        return acc.reshape(group, block, chans)

    def second_back(g, carry):
        d = back(sc, g, m2)
        for n in range(group):
            r = g * group + n
            put(sa, r, jnp.where(live, d[n] * slope1[r], 0.0))
        return carry

    lax.fori_loop(0, regions // group, second_back, 0)

    def first_back(g, carry):
        d = back(sa, g, m1)
        for n in range(group):
            cg[g * group + n] = d[n].astype(jnp.bfloat16)
        return carry

    lax.fori_loop(0, regions // group, first_back, 0)

    total = None
    for r in range(regions):
        term = dot(mt[r], cg[r])
        total = term if total is None else total + term
    for c in range(2):
        part[c] = total[:, c * half : (c + 1) * half]
    sum_copy = pltpu.make_async_remote_copy(
        src_ref=part.at[1 - chan],
        dst_ref=part_got,
        send_sem=part_sem.at[0],
        recv_sem=part_sem.at[1],
        device_id=near(0, 0, 1),
        device_id_type=MESH,
    )
    sum_copy.start()

    def wait_mask(d, carry):
        block_copy(mask_out, mask_got, mask_send, mask_recv, d).wait()
        return carry

    lax.fori_loop(1, peers, wait_mask, 0)

    def place_one(n, carry):
        def look(at, found):
            return jnp.where(table[at] == n, at, found)

        at = lax.fori_loop(0, peers * per_core, look, jnp.int32(-1))
        at0 = jnp.maximum(at, 0)
        got = mask_got[at0 // per_core, at0 % per_core][:, 0:samples, :]
        mask_ref[n] = jnp.where(at >= 0, got, jnp.zeros_like(got))
        return carry

    lax.fori_loop(0, capacity, place_one, 0)
    sum_copy.wait()
    grad_ref[...] = (part[chan] + part_got[...]).reshape(rows, width, half).astype(grad_ref.dtype)
    for at, (dy, dx, dc) in enumerate(OFFSETS):

        @pl.when(there(dy, dx))
        def _():
            halo(at).wait_send()

    for copy in weights:
        copy.wait_send()


def shards(
    features, tile_first, tile_second, mask_first, mask_second, region_boxes, owner_strip, cotangent
):
    rows, width, half = features.shape
    chans = 2 * half
    capacity, samples = (cotangent.shape[2], cotangent.shape[3])
    block = samples * EDGE
    strips, cols = (lax.axis_size("strip"), lax.axis_size("col"))
    slots = owner_strip.shape[2]
    regions = slots // 2
    per_core = -(-(-(-capacity // strips)) // 2)
    peers = 2 * strips
    prows, pwidth = (rows + 4, width + 2 * EDGE)
    group = 2
    vmem = pl.BlockSpec(memory_space=pltpu.VMEM)
    smem = pl.BlockSpec(memory_space=pltpu.SMEM)
    weights = [w.reshape(3, 3 * chans, half) for w in (tile_first, tile_second, mask_first, mask_second)]
    bf16, f32, i32 = (jnp.bfloat16, jnp.float32, jnp.int32)
    sem = pltpu.SemaphoreType.DMA
    blocks = pltpu.VMEM((peers, per_core, samples, EDGE, half), bf16)
    stack = pltpu.VMEM((regions, block + 2 * EDGE, 3 * chans), bf16)
    slope = pltpu.VMEM((regions, block, chans), f32)
    mask_out, grad_tile = pl.pallas_call(
        functools.partial(head_kernel, strips, cols, group),
        out_shape=[
            jax.ShapeDtypeStruct((capacity, samples, samples, half), bf16),
            jax.ShapeDtypeStruct((rows, width, half), bf16),
        ],
        in_specs=[smem, smem] + [vmem] * 7,
        out_specs=[vmem, vmem],
        scratch_shapes=[pltpu.VMEM((2, prows, pwidth, half), bf16)]
        + [pltpu.VMEM((2, 3, 3 * chans, half), bf16)] * 4
        + [
            pltpu.VMEM((8, 128), i32),
            pltpu.VMEM((strips, 8, 128), i32),
            pltpu.SMEM((strips, 8, 128), i32),
            pltpu.SMEM((peers * per_core,), i32),
        ]
        + [blocks] * 4
        + [
            pltpu.VMEM((2, rows * width, half), f32),
            pltpu.VMEM((rows * width, half), f32),
            pltpu.VMEM((prows * pwidth, 3 * chans), bf16),
            pltpu.VMEM(((prows - 2) * pwidth, 3 * chans), bf16),
            pltpu.VMEM((rows * width, chans), bf16),
            stack,
            stack,
            slope,
            slope,
            pltpu.VMEM((regions, block, chans), bf16),
            pltpu.VMEM((regions, rows * width, block), bf16),
            pltpu.VMEM((regions, block, chans), bf16),
        ]
        + [sem((len(OFFSETS),))] * 2
        + [sem((4,))] * 2
        + [sem((strips,))] * 2
        + [sem((peers,))] * 4
        + [sem((2,)), sem((6,))],
        compiler_params=pltpu.CompilerParams(
            collective_id=0, has_side_effects=True, vmem_limit_bytes=VMEM_BYTES
        ),
        name="head",
    )(region_boxes[0, 0], owner_strip[0, 0], owner_strip[0], features, *weights, cotangent[0, 0])
    return (mask_out[None, None], grad_tile)


def solution(mesh):
    placed = (
        P(("grp", "strip"), "col", "chan"),
        P(None, None, None, "chan"),
        P(None, None, None, "chan"),
        P(None, None, None, "chan"),
        P(None, None, None, "chan"),
        P(("grp", "strip"), "col", None, None),
        P(("grp", "strip"), "col", None),
        P(("grp", "strip"), "col", None, None, None, "chan"),
    )
    return jax.shard_map(
        shards,
        mesh=mesh,
        in_specs=placed,
        out_specs=(
            P(("grp", "strip"), "col", None, None, None, "chan"),
            P(("grp", "strip"), "col", "chan"),
        ),
        check_vma=False,
    )
```

```python
import functools

import jax
import jax.numpy as jnp
from jax import lax
from jax.experimental import pallas as pl
from jax.experimental.pallas import tpu as pltpu
from jax.sharding import PartitionSpec as P

MESH = pl.DeviceIdType.MESH
VMEM_BYTES = 56 * 1024 * 1024
EDGE = 16
OFFSETS = [(dy, dx, dc) for dy in (0, -1, 1) for dx in (0, -1, 1) for dc in (1, 0) if (dy, dx, dc) != (0, 0, 0)]


def sigmoid(v):
    return 1.0 / (1.0 + jnp.exp(-v))


def taps(v):
    count = v.shape[0]
    return (pltpu.roll(v, 1, 0), v, pltpu.roll(v, count - 1, 0))


def dot(a, b):
    return jnp.dot(a, b, preferred_element_type=jnp.float32)


def dot_t(a, b):
    return lax.dot_general(a, b, (((1,), (1,)), ((), ())), preferred_element_type=jnp.float32)


def both(w, a, rows=slice(None)):
    return jnp.concatenate([w[0, a, rows, :], w[1, a, rows, :]], axis=-1)


def sample_weight(start, length, index, cell, samples):
    twice = 2 * samples
    num = twice * start + (2 * index + 1) * length - samples
    last = start + length - 1
    num = jnp.minimum(jnp.maximum(num, twice * start), twice * last)
    low = (num * 2341) >> 16
    frac = (num - twice * low).astype(jnp.float32) / twice
    high = jnp.minimum(low + 1, last)
    return jnp.where(cell == low, 1.0 - frac, 0.0) + jnp.where(cell == high, frac, 0.0)


def head_kernel(
    strips,
    cols,
    group,
    samples,
    boxes,
    owners,
    owner_row,
    f_ref,
    w0,
    w1,
    w2,
    w3,
    cot_in,
    mask_ref,
    grad_ref,
    pad_ref,
    t1,
    t2,
    m1,
    m2,
    own_tile,
    all_tile,
    all_owner,
    table,
    order,
    seat,
    cot_out,
    cot_got,
    mask_out,
    mask_got,
    part,
    part_got,
    s0,
    s1,
    feat,
    sc,
    sa,
    slope1,
    slope2,
    mask_own,
    pack,
    mt,
    cg,
    halo_send,
    halo_recv,
    weight_send,
    weight_recv,
    owner_send,
    owner_recv,
    cot_send,
    cot_recv,
    mask_send,
    mask_recv,
    part_sem,
    own_sem,
):
    strip, col, chan = (lax.axis_index("strip"), lax.axis_index("col"), lax.axis_index("chan"))
    rows, width, half = f_ref.shape
    chans = 2 * half
    capacity, area = (mask_ref.shape[0], mask_ref.shape[1])
    regions = slope1.shape[0]
    per_core, packed = (pack.shape[0], pack.shape[1])
    prows, pwidth = (pad_ref.shape[1], pad_ref.shape[2])
    block = samples * EDGE
    peers = 2 * strips
    me = strip * 2 + chan

    def there(dy, dx):
        return (strip + dy >= 0) & (strip + dy < strips) & (col + dx >= 0) & (col + dx < cols)

    def near(dy, dx, dc):
        return {"strip": strip + dy, "col": col + dx, "chan": (chan + dc) % 2}

    def peer(d):
        other = lax.rem(me + d, peers)
        return {"strip": other // 2, "chan": lax.rem(other, 2)}

    barrier = pltpu.get_barrier_semaphore()
    for dy, dx, dc in OFFSETS:
        if dx != 0:

            @pl.when(there(dy, dx))
            def _():
                pl.semaphore_signal(barrier, inc=1, device_id=near(dy, dx, dc), device_id_type=MESH)

    def greet(d, carry):
        pl.semaphore_signal(barrier, inc=1, device_id=peer(d), device_id_type=MESH)
        return carry

    lax.fori_loop(1, peers, greet, 0)
    near_rows = 1 + jnp.where(strip > 0, 1, 0) + jnp.where(strip < strips - 1, 1, 0)
    near_cols = jnp.where(col > 0, 1, 0) + jnp.where(col < cols - 1, 1, 0)
    own_tile[...] = jnp.zeros_like(own_tile)
    own_tile[0:1, 0 : owner_row.shape[1]] = owner_row[...]
    pl.semaphore_wait(barrier, 2 * near_rows * near_cols + peers - 1)

    def owner_copy(d):
        return pltpu.make_async_remote_copy(
            src_ref=own_tile,
            dst_ref=all_tile.at[strip],
            send_sem=owner_send.at[d],
            recv_sem=owner_recv.at[d],
            device_id={"strip": lax.rem(strip + d, strips)},
            device_id_type=MESH,
        )

    def start_owner(d, carry):
        owner_copy(d).start()
        return carry

    lax.fori_loop(1, strips, start_owner, 0)

    row_from = {0: (0, rows), 1: (rows - 2, 2), -1: (0, 2)}
    row_to = {0: 2, 1: 0, -1: rows + 2}
    col_from = {0: (0, width), 1: (width - EDGE, EDGE), -1: (0, EDGE)}
    col_to = {0: EDGE, 1: 0, -1: width + EDGE}

    def halo(at):
        dy, dx, dc = OFFSETS[at]
        row, row_count = row_from[dy]
        first, count = col_from[dx]
        return pltpu.make_async_remote_copy(
            src_ref=f_ref.at[pl.ds(row, row_count), pl.ds(first, count)],
            dst_ref=pad_ref.at[chan, pl.ds(row_to[dy], row_count), pl.ds(col_to[dx], count)],
            send_sem=halo_send.at[at],
            recv_sem=halo_recv.at[at],
            device_id=near(dy, dx, dc),
            device_id_type=MESH,
        )

    pairs = ((w0, t1), (w1, t2), (w2, m1), (w3, m2))
    weights = [
        pltpu.make_async_remote_copy(
            src_ref=w,
            dst_ref=o.at[chan],
            send_sem=weight_send.at[i],
            recv_sem=weight_recv.at[i],
            device_id=near(0, 0, 1),
            device_id_type=MESH,
        )
        for i, (w, o) in enumerate(pairs)
    ]
    for at, (dy, dx, dc) in enumerate(OFFSETS):

        @pl.when(there(dy, dx))
        def _():
            halo(at).start()

    for copy in weights:
        copy.start()
    own = [pltpu.make_async_copy(w, o.at[chan], own_sem.at[i]) for i, (w, o) in enumerate(pairs)]
    own.append(
        pltpu.make_async_copy(f_ref, pad_ref.at[chan, pl.ds(2, rows), pl.ds(EDGE, width)], own_sem.at[4])
    )
    for copy in own:
        copy.start()

    all_tile[strip] = own_tile[...]

    def clear(i, carry):
        cot_out[i] = jnp.zeros(cot_out.shape[1:], cot_out.dtype)
        return carry

    lax.fori_loop(0, peers, clear, 0)

    def wait_owner(d, carry):
        owner_copy(d).wait()
        return carry

    lax.fori_loop(1, strips, wait_owner, 0)
    to_scalar = pltpu.make_async_copy(all_tile, all_owner, own_sem.at[5])
    to_scalar.start()
    to_scalar.wait()

    def find(s, number):
        for core in range(2):
            for p in range(per_core):
                table[(2 * s + core) * per_core + p] = jnp.int32(-1)
        seen = [jnp.int32(0), jnp.int32(0)]
        held = [[jnp.int32(-1)] * per_core, [jnp.int32(-1)] * per_core]
        for at in range(2 * regions):
            core = at % 2
            hit = all_owner[s, 0, at] == strip
            for p in range(per_core):
                held[core][p] = jnp.where(hit & (seen[core] == p), number, held[core][p])
            one = jnp.where(hit, 1, 0)
            seen[core] = seen[core] + one
            number = number + one
        for core in range(2):
            for p in range(per_core):
                table[(2 * s + core) * per_core + p] = held[core][p]
        return number

    lax.fori_loop(0, strips, find, jnp.int32(0))

    raw = [owners[2 * r + chan] for r in range(regions)]
    key = [lax.rem(o - strip - 1 + 2 * strips, strips) for o in raw]
    spot = []
    for r in range(regions):
        ahead = jnp.int32(0)
        for other in range(regions):
            if other != r:
                less = key[other] <= key[r] if other < r else key[other] < key[r]
                ahead = ahead + jnp.where(less, 1, 0)
        spot.append(ahead)
    mine = []
    for x in range(regions):
        found = jnp.int32(0)
        for r in range(regions):
            found = jnp.where(spot[r] == x, r, found)
        order[x] = 2 * found + chan
        mine.append(owners[2 * found + chan])
    rank = []
    for r in range(regions):
        total = jnp.int32(0)
        for before in range(r):
            total = total + jnp.where(mine[before] == mine[r], 1, 0)
        rank.append(total)
    for r in range(regions):
        seat[r] = 2 * per_core * mine[r] + jnp.minimum(rank[r], per_core - 1)

    def choose(i, carry):
        for p in range(per_core):
            slot = jnp.clip(table[i * per_core + p], 0, capacity - 1)
            cot_out[i, p * area : (p + 1) * area, :] = cot_in[slot]
        return carry

    lax.fori_loop(0, peers, choose, 0)

    def block_copy(src, dst, send, recv, d):
        return pltpu.make_async_remote_copy(
            src_ref=src.at[lax.rem(me + d, peers)],
            dst_ref=dst.at[me],
            send_sem=send.at[d],
            recv_sem=recv.at[d],
            device_id=peer(d),
            device_id_type=MESH,
        )

    def start_cot(d, carry):
        block_copy(cot_out, cot_got, cot_send, cot_recv, d).start()
        return carry

    lax.fori_loop(1, peers, start_cot, 0)
    cot_got[me] = cot_out[me]

    for copy in own:
        copy.wait()
    for at, (dy, dx, dc) in enumerate(OFFSETS):

        @pl.when(there(-dy, -dx))
        def _():
            halo(at).wait_recv()

    weights[0].wait_recv()
    top_ok, bottom_ok = (strip > 0, strip < strips - 1)
    x_ids = lax.broadcasted_iota(jnp.int32, (pwidth, 1), 0)
    x_lo = jnp.where(col > 0, 0, EDGE)
    x_hi = jnp.where(col < cols - 1, pwidth, EDGE + width)
    x_ok = (x_ids >= x_lo) & (x_ids < x_hi)

    def fill_row(y, carry):
        y_lo = jnp.where(top_ok, 0, 2)
        y_hi = jnp.where(bottom_ok, prows, prows - 2)
        ok = x_ok & (y >= y_lo) & (y < y_hi)
        for c in range(2):
            v = jnp.where(ok, pad_ref[c, y].astype(jnp.float32), 0.0)
            for b, t in enumerate(taps(v)):
                at = b * chans + c * half
                s0[pl.ds(y * pwidth, pwidth), at : at + half] = t.astype(jnp.bfloat16)
        return carry

    lax.fori_loop(0, prows, fill_row, 0, unroll=4)

    hid_rows = prows - 2
    step = 6
    size = step * pwidth
    ids = lax.broadcasted_iota(jnp.int32, (size, 1), 0)
    sub_row = ids // pwidth
    sub_col = ids % pwidth

    def hidden_chunk(i, carry):
        acc = None
        for a in range(3):
            term = dot(s0[pl.ds(pl.multiple_of((i * step + a) * pwidth, pwidth), size), :], both(t1, a))
            acc = term if acc is None else acc + term
        y = sub_row + i * step
        y_lo = jnp.where(top_ok, 0, 1)
        y_hi = jnp.where(bottom_ok, hid_rows, hid_rows - 1)
        ok = (sub_col >= x_lo) & (sub_col < x_hi) & (y >= y_lo) & (y < y_hi)
        v = jnp.where(ok, acc * sigmoid(acc), 0.0)
        for b, t in enumerate(taps(v)):
            s1[pl.ds(pl.multiple_of(i * size, size), size), b * chans : (b + 1) * chans] = t.astype(jnp.bfloat16)
        return carry

    lax.fori_loop(0, hid_rows // step, hidden_chunk, 0)

    weights[1].wait_recv()
    fstep = 8
    fsize = fstep * pwidth

    def feat_chunk(i, carry):
        acc = None
        for a in range(3):
            term = dot(s1[pl.ds(pl.multiple_of((i * fstep + a) * pwidth, pwidth), fsize), :], both(t2, a))
            acc = term if acc is None else acc + term
        v = (acc * sigmoid(acc)).reshape(fstep, pwidth, chans)[:, EDGE : EDGE + width, :]
        feat[pl.ds(pl.multiple_of(i * fstep * width, fstep * width), fstep * width), :] = v.reshape(
            fstep * width, chans
        ).astype(jnp.bfloat16)
        return carry

    lax.fori_loop(0, rows // fstep, feat_chunk, 0)

    block = samples * EDGE
    p = lax.broadcasted_iota(jnp.int32, (block, 1), 0)
    i_id, k_id = (p // EDGE, p % EDGE)
    q = lax.broadcasted_iota(jnp.int32, (1, rows * width), 1)
    y_id, x_id = (q // width, q % width)
    live = k_id < samples
    zeros = jnp.zeros((EDGE, 3 * chans), jnp.bfloat16)

    def put(dst, r, v):
        for b, t in enumerate(taps(v)):
            dst[r, EDGE : EDGE + block, b * chans : (b + 1) * chans] = t.astype(jnp.bfloat16)

    def crop_one(r, carry):
        row = sample_weight(boxes[0, order[r]] - strip * rows, boxes[2, order[r]], i_id, y_id, samples)
        column = sample_weight(boxes[1, order[r]] - col * width, boxes[3, order[r]], k_id, x_id, samples)
        weight = jnp.where(live, row * column, 0.0).astype(jnp.bfloat16)
        put(sc, r, dot(weight, feat[...]))
        for dst in (sc, sa):
            dst[r, 0:EDGE, :] = zeros
            dst[r, EDGE + block : 2 * EDGE + block, :] = zeros
        return carry

    lax.fori_loop(0, regions, crop_one, 0)

    def conv(src, g, w):
        acc = None
        for a in range(3):
            lhs = src[pl.ds(g * group, group), a * EDGE : a * EDGE + block, :].reshape(group * block, 3 * chans)
            term = dot(lhs, both(w, a))
            acc = term if acc is None else acc + term
        return acc.reshape(group, block, chans)

    weights[2].wait_recv()
    weights[3].wait_recv()

    def first_layer(g, carry):
        pre = conv(sc, g, m1)
        for n in range(group):
            v = pre[n]
            s = sigmoid(v)
            slope1[g * group + n] = s * (1.0 + v * (1.0 - s))
            put(sa, g * group + n, jnp.where(live, v * s, 0.0))
        return carry

    def second_layer(g, carry):
        pre = conv(sa, g, m2)
        for n in range(group):
            r = g * group + n
            v = pre[n]
            s = sigmoid(v)
            slope2[r] = s * (1.0 + v * (1.0 - s))
            mask_own[r] = (v * s).astype(jnp.bfloat16)
        return carry

    row_id = lax.broadcasted_iota(jnp.int32, (packed, 1), 0)
    lane_id = lax.broadcasted_iota(jnp.int32, (1, block), 1)
    for p in range(per_core):
        local = row_id - p * area
        line = (local * 4682) >> 16
        cell = line * EDGE + local - line * samples
        hit = (local >= 0) & (local < area) & (cell == lane_id)
        pack[p] = jnp.where(hit, 1.0, 0.0).astype(jnp.bfloat16)

    def gather_mask(d, carry):
        o = lax.rem(strip + 1 + d, strips)
        for p in range(per_core):
            pick = jnp.int32(0)
            for r in range(regions):
                pick = jnp.where((mine[r] == o) & (rank[r] == p), r, pick)
            term = dot(pack[p], mask_own[pick])
            out = term if p == 0 else out + term
        for c in range(2):
            mask_out[2 * o + c] = out[:, c * half : (c + 1) * half].astype(jnp.bfloat16)
        for c in range(2):
            away = lax.rem(2 * o + c - me + peers, peers)

            @pl.when(away > 0)
            def _():
                block_copy(mask_out, mask_got, mask_send, mask_recv, away).start()

        return carry

    groups = regions // group

    def layers(g, carry):
        first_layer(g, carry)
        second_layer(g, carry)
        done = jnp.where(g == groups - 1, strips, jnp.minimum((g + 1) * group // per_core, strips - 1))
        lax.fori_loop(jnp.minimum(g * group // per_core, strips - 1), done, gather_mask, 0)
        return carry

    lax.fori_loop(0, groups, layers, 0)
    mask_got[me] = mask_out[me]

    def wait_cot(d, carry):
        block_copy(cot_out, cot_got, cot_send, cot_recv, d).wait()
        return carry

    lax.fori_loop(1, peers, wait_cot, 0)

    yt = lax.broadcasted_iota(jnp.int32, (rows * width, 1), 0)
    yt_id, xt_id = (yt // width, yt % width)
    pt = lax.broadcasted_iota(jnp.int32, (1, block), 1)
    it_id, kt_id = (pt // EDGE, pt % EDGE)

    packed_id = lax.broadcasted_iota(jnp.int32, (1, packed), 1)

    def start_grad(r, carry):
        at_seat = seat[r]
        owner = at_seat // (2 * per_core)
        place = lax.rem(at_seat, 2 * per_core)
        taken = place * area + i_id * samples + k_id
        spread = jnp.where(live & (taken == packed_id), 1.0, 0.0).astype(jnp.bfloat16)
        cot = dot(spread, jnp.concatenate([cot_got[2 * owner], cot_got[2 * owner + 1]], axis=-1))
        put(sc, r, cot * slope2[r])
        row = sample_weight(
            boxes[0, order[r]] - strip * rows, boxes[2, order[r]], it_id, yt_id, samples
        )
        column = sample_weight(
            boxes[1, order[r]] - col * width, boxes[3, order[r]], kt_id, xt_id, samples
        )
        mt[r] = jnp.where(kt_id < samples, row * column, 0.0).astype(jnp.bfloat16)
        return carry

    lax.fori_loop(0, regions, start_grad, 0)

    def back(src, g, w):
        acc = None
        for a in range(3):
            for b in range(3):
                lhs = src[
                    pl.ds(g * group, group), a * EDGE : a * EDGE + block, b * chans : (b + 1) * chans
                ].reshape(group * block, chans)
                term = dot_t(lhs, both(w, 2 - a, slice((2 - b) * chans, (3 - b) * chans)))
                acc = term if acc is None else acc + term
        return acc.reshape(group, block, chans)

    def second_back(g, carry):
        d = back(sc, g, m2)
        for n in range(group):
            r = g * group + n
            put(sa, r, jnp.where(live, d[n] * slope1[r], 0.0))
        return carry

    lax.fori_loop(0, regions // group, second_back, 0)

    def first_back(g, carry):
        d = back(sa, g, m1)
        for n in range(group):
            cg[g * group + n] = d[n].astype(jnp.bfloat16)
        return carry

    lax.fori_loop(0, regions // group, first_back, 0)

    total = None
    for r in range(regions):
        term = dot(mt[r], cg[r])
        total = term if total is None else total + term
    for c in range(2):
        part[c] = total[:, c * half : (c + 1) * half]
    sum_copy = pltpu.make_async_remote_copy(
        src_ref=part.at[1 - chan],
        dst_ref=part_got,
        send_sem=part_sem.at[0],
        recv_sem=part_sem.at[1],
        device_id=near(0, 0, 1),
        device_id_type=MESH,
    )
    sum_copy.start()

    def wait_mask(d, carry):
        block_copy(mask_out, mask_got, mask_send, mask_recv, d).wait()
        return carry

    lax.fori_loop(1, peers, wait_mask, 0)

    def place_one(n, carry):
        def look(at, found):
            return jnp.where(table[at] == n, at, found)

        at = lax.fori_loop(0, peers * per_core, look, jnp.int32(-1))
        at0 = jnp.maximum(at, 0)
        got = mask_got[at0 // per_core, 0:area, :]
        for p in range(1, per_core):
            got = jnp.where(at0 % per_core == p, mask_got[at0 // per_core, p * area : (p + 1) * area, :], got)
        mask_ref[n] = jnp.where(at >= 0, got, jnp.zeros_like(got))
        return carry

    lax.fori_loop(0, capacity, place_one, 0)
    sum_copy.wait()
    grad_ref[...] = (part[chan] + part_got[...]).reshape(rows, width, half).astype(grad_ref.dtype)
    for at, (dy, dx, dc) in enumerate(OFFSETS):

        @pl.when(there(dy, dx))
        def _():
            halo(at).wait_send()

    for copy in weights:
        copy.wait_send()


def shards(
    features, tile_first, tile_second, mask_first, mask_second, region_boxes, owner_strip, cotangent
):
    rows, width, half = features.shape
    chans = 2 * half
    capacity, samples = (cotangent.shape[2], cotangent.shape[3])
    block = samples * EDGE
    strips, cols = (lax.axis_size("strip"), lax.axis_size("col"))
    slots = owner_strip.shape[2]
    regions = slots // 2
    per_core = -(-(-(-capacity // strips)) // 2)
    peers = 2 * strips
    prows, pwidth = (rows + 4, width + 2 * EDGE)
    group = 2
    vmem = pl.BlockSpec(memory_space=pltpu.VMEM)
    smem = pl.BlockSpec(memory_space=pltpu.SMEM)
    weights = [w.reshape(3, 3 * chans, half) for w in (tile_first, tile_second, mask_first, mask_second)]
    bf16, f32, i32 = (jnp.bfloat16, jnp.float32, jnp.int32)
    sem = pltpu.SemaphoreType.DMA
    area = samples * samples
    packed = -(-per_core * area // EDGE) * EDGE
    blocks = pltpu.VMEM((peers, packed, half), bf16)
    stack = pltpu.VMEM((regions, block + 2 * EDGE, 3 * chans), bf16)
    slope = pltpu.VMEM((regions, block, chans), f32)
    mask_out, grad_tile = pl.pallas_call(
        functools.partial(head_kernel, strips, cols, group, samples),
        out_shape=[
            jax.ShapeDtypeStruct((capacity, area, half), bf16),
            jax.ShapeDtypeStruct((rows, width, half), bf16),
        ],
        in_specs=[smem, smem] + [vmem] * 7,
        out_specs=[vmem, vmem],
        scratch_shapes=[pltpu.VMEM((2, prows, pwidth, half), bf16)]
        + [pltpu.VMEM((2, 3, 3 * chans, half), bf16)] * 4
        + [
            pltpu.VMEM((8, 128), i32),
            pltpu.VMEM((strips, 8, 128), i32),
            pltpu.SMEM((strips, 8, 128), i32),
            pltpu.SMEM((peers * per_core,), i32),
            pltpu.SMEM((regions,), i32),
            pltpu.SMEM((regions,), i32),
        ]
        + [blocks] * 4
        + [
            pltpu.VMEM((2, rows * width, half), f32),
            pltpu.VMEM((rows * width, half), f32),
            pltpu.VMEM((prows * pwidth, 3 * chans), bf16),
            pltpu.VMEM(((prows - 2) * pwidth, 3 * chans), bf16),
            pltpu.VMEM((rows * width, chans), bf16),
            stack,
            stack,
            slope,
            slope,
            pltpu.VMEM((regions, block, chans), bf16),
            pltpu.VMEM((per_core, packed, block), bf16),
            pltpu.VMEM((regions, rows * width, block), bf16),
            pltpu.VMEM((regions, block, chans), bf16),
        ]
        + [sem((len(OFFSETS),))] * 2
        + [sem((4,))] * 2
        + [sem((strips,))] * 2
        + [sem((peers,))] * 4
        + [sem((2,)), sem((6,))],
        compiler_params=pltpu.CompilerParams(
            collective_id=0, has_side_effects=True, vmem_limit_bytes=VMEM_BYTES
        ),
        name="head",
    )(region_boxes[0, 0].T, owner_strip[0, 0], owner_strip[0], features, *weights, cotangent.reshape(capacity, area, half))
    return (mask_out.reshape(cotangent.shape), grad_tile)


def solution(mesh):
    placed = (
        P(("grp", "strip"), "col", "chan"),
        P(None, None, None, "chan"),
        P(None, None, None, "chan"),
        P(None, None, None, "chan"),
        P(None, None, None, "chan"),
        P(("grp", "strip"), "col", None, None),
        P(("grp", "strip"), "col", None),
        P(("grp", "strip"), "col", None, None, None, "chan"),
    )
    return jax.shard_map(
        shards,
        mesh=mesh,
        in_specs=placed,
        out_specs=(
            P(("grp", "strip"), "col", None, None, None, "chan"),
            P(("grp", "strip"), "col", "chan"),
        ),
        check_vma=False,
    )
```

```python
import functools

import jax
import jax.numpy as jnp
from jax import lax
from jax.experimental import pallas as pl
from jax.experimental.pallas import tpu as pltpu
from jax.sharding import PartitionSpec as P

MESH = pl.DeviceIdType.MESH
VMEM_BYTES = 56 * 1024 * 1024
EDGE = 16
OFFSETS = [(dy, dx, dc) for dy in (0, -1, 1) for dx in (0, -1, 1) for dc in (1, 0) if (dy, dx, dc) != (0, 0, 0)]


def sigmoid(v):
    return 1.0 / (1.0 + jnp.exp(-v))


def taps(v):
    count = v.shape[0]
    return (pltpu.roll(v, 1, 0), v, pltpu.roll(v, count - 1, 0))


def dot(a, b):
    return jnp.dot(a, b, preferred_element_type=jnp.float32)


def dot_t(a, b):
    return lax.dot_general(a, b, (((1,), (1,)), ((), ())), preferred_element_type=jnp.float32)


def both(w, a, rows=slice(None)):
    return jnp.concatenate([w[0, a, rows, :], w[1, a, rows, :]], axis=-1)


def sample_weight(start, length, index, cell, samples):
    twice = 2 * samples
    num = twice * start + (2 * index + 1) * length - samples
    last = start + length - 1
    num = jnp.minimum(jnp.maximum(num, twice * start), twice * last)
    low = (num * 2341) >> 16
    frac = (num - twice * low).astype(jnp.float32) / twice
    high = jnp.minimum(low + 1, last)
    return jnp.where(cell == low, 1.0 - frac, 0.0) + jnp.where(cell == high, frac, 0.0)


def head_kernel(
    strips,
    cols,
    group,
    samples,
    boxes,
    owners,
    owner_row,
    f_ref,
    w0,
    w1,
    w2,
    w3,
    cot_in,
    mask_ref,
    grad_ref,
    pad_ref,
    t1,
    t2,
    m1,
    m2,
    own_tile,
    all_tile,
    all_owner,
    table,
    order,
    seat,
    cot_out,
    cot_got,
    mask_out,
    mask_got,
    part,
    part_got,
    s0,
    s1,
    feat,
    sc,
    sa,
    slope1,
    slope2,
    mask_own,
    pack,
    mt,
    cg,
    halo_send,
    halo_recv,
    weight_send,
    weight_recv,
    owner_send,
    owner_recv,
    cot_send,
    cot_recv,
    mask_send,
    mask_recv,
    part_sem,
    own_sem,
):
    strip, col, chan = (lax.axis_index("strip"), lax.axis_index("col"), lax.axis_index("chan"))
    rows, width, half = f_ref.shape
    chans = 2 * half
    capacity, area = (mask_ref.shape[0], mask_ref.shape[1])
    regions = slope1.shape[0]
    per_core, packed = (pack.shape[0], pack.shape[1])
    prows, pwidth = (pad_ref.shape[1], pad_ref.shape[2])
    block = samples * EDGE
    peers = 2 * strips
    me = strip * 2 + chan
    base = jnp.where(strip < strips // 2, strips // 2, 0)

    def there(dy, dx):
        return (strip + dy >= 0) & (strip + dy < strips) & (col + dx >= 0) & (col + dx < cols)

    def near(dy, dx, dc):
        return {"strip": strip + dy, "col": col + dx, "chan": (chan + dc) % 2}

    def peer(d):
        other = lax.rem(me + d, peers)
        return {"strip": other // 2, "chan": lax.rem(other, 2)}

    barrier = pltpu.get_barrier_semaphore()
    for dy, dx, dc in OFFSETS:
        if dx != 0:

            @pl.when(there(dy, dx))
            def _():
                pl.semaphore_signal(barrier, inc=1, device_id=near(dy, dx, dc), device_id_type=MESH)

    def greet(d, carry):
        pl.semaphore_signal(barrier, inc=1, device_id=peer(d), device_id_type=MESH)
        return carry

    lax.fori_loop(1, peers, greet, 0)
    near_rows = 1 + jnp.where(strip > 0, 1, 0) + jnp.where(strip < strips - 1, 1, 0)
    near_cols = jnp.where(col > 0, 1, 0) + jnp.where(col < cols - 1, 1, 0)
    own_tile[...] = jnp.zeros_like(own_tile)
    own_tile[0:1, 0 : owner_row.shape[1]] = owner_row[...]
    pl.semaphore_wait(barrier, 2 * near_rows * near_cols + peers - 1)

    def owner_copy(d):
        return pltpu.make_async_remote_copy(
            src_ref=own_tile,
            dst_ref=all_tile.at[strip],
            send_sem=owner_send.at[d],
            recv_sem=owner_recv.at[d],
            device_id={"strip": lax.rem(strip + d, strips)},
            device_id_type=MESH,
        )

    def start_owner(d, carry):
        owner_copy(d).start()
        return carry

    lax.fori_loop(1, strips, start_owner, 0)

    row_from = {0: (0, rows), 1: (rows - 2, 2), -1: (0, 2)}
    row_to = {0: 2, 1: 0, -1: rows + 2}
    col_from = {0: (0, width), 1: (width - EDGE, EDGE), -1: (0, EDGE)}
    col_to = {0: EDGE, 1: 0, -1: width + EDGE}

    def halo(at):
        dy, dx, dc = OFFSETS[at]
        row, row_count = row_from[dy]
        first, count = col_from[dx]
        return pltpu.make_async_remote_copy(
            src_ref=f_ref.at[pl.ds(row, row_count), pl.ds(first, count)],
            dst_ref=pad_ref.at[chan, pl.ds(row_to[dy], row_count), pl.ds(col_to[dx], count)],
            send_sem=halo_send.at[at],
            recv_sem=halo_recv.at[at],
            device_id=near(dy, dx, dc),
            device_id_type=MESH,
        )

    pairs = ((w0, t1), (w1, t2), (w2, m1), (w3, m2))
    weights = [
        pltpu.make_async_remote_copy(
            src_ref=w,
            dst_ref=o.at[chan],
            send_sem=weight_send.at[i],
            recv_sem=weight_recv.at[i],
            device_id=near(0, 0, 1),
            device_id_type=MESH,
        )
        for i, (w, o) in enumerate(pairs)
    ]
    for at, (dy, dx, dc) in enumerate(OFFSETS):

        @pl.when(there(dy, dx))
        def _():
            halo(at).start()

    for copy in weights:
        copy.start()
    own = [pltpu.make_async_copy(w, o.at[chan], own_sem.at[i]) for i, (w, o) in enumerate(pairs)]
    own.append(
        pltpu.make_async_copy(f_ref, pad_ref.at[chan, pl.ds(2, rows), pl.ds(EDGE, width)], own_sem.at[4])
    )
    for copy in own:
        copy.start()

    all_tile[strip] = own_tile[...]

    def clear(i, carry):
        cot_out[i] = jnp.zeros(cot_out.shape[1:], cot_out.dtype)
        return carry

    lax.fori_loop(0, peers, clear, 0)

    def wait_owner(d, carry):
        owner_copy(d).wait()
        return carry

    lax.fori_loop(1, strips, wait_owner, 0)
    to_scalar = pltpu.make_async_copy(all_tile, all_owner, own_sem.at[5])
    to_scalar.start()
    to_scalar.wait()

    def find(s, number):
        for core in range(2):
            for p in range(per_core):
                table[(2 * s + core) * per_core + p] = jnp.int32(-1)
        seen = [jnp.int32(0), jnp.int32(0)]
        held = [[jnp.int32(-1)] * per_core, [jnp.int32(-1)] * per_core]
        for at in range(2 * regions):
            core = at % 2
            hit = all_owner[s, 0, at] == strip
            for p in range(per_core):
                held[core][p] = jnp.where(hit & (seen[core] == p), number, held[core][p])
            one = jnp.where(hit, 1, 0)
            seen[core] = seen[core] + one
            number = number + one
        for core in range(2):
            for p in range(per_core):
                table[(2 * s + core) * per_core + p] = held[core][p]
        return number

    lax.fori_loop(0, strips, find, jnp.int32(0))

    def block_copy(src, dst, send, recv, d):
        return pltpu.make_async_remote_copy(
            src_ref=src.at[lax.rem(me + d, peers)],
            dst_ref=dst.at[me],
            send_sem=send.at[d],
            recv_sem=recv.at[d],
            device_id=peer(d),
            device_id_type=MESH,
        )

    def send_cot(i, carry):
        to = lax.rem(2 * base + i, peers)
        for p in range(per_core):
            slot = jnp.clip(table[to * per_core + p], 0, capacity - 1)
            cot_out[to, p * area : (p + 1) * area, :] = cot_in[slot]
        away = lax.rem(to - me + peers, peers)

        @pl.when(away > 0)
        def _():
            block_copy(cot_out, cot_got, cot_send, cot_recv, away).start()

        return carry

    lax.fori_loop(0, peers, send_cot, 0)
    cot_got[me] = cot_out[me]

    raw = [owners[2 * r + chan] for r in range(regions)]
    key = [lax.rem(o - base + strips, strips) for o in raw]
    spot = []
    for r in range(regions):
        ahead = jnp.int32(0)
        for other in range(regions):
            if other != r:
                less = key[other] <= key[r] if other < r else key[other] < key[r]
                ahead = ahead + jnp.where(less, 1, 0)
        spot.append(ahead)
    mine = []
    for x in range(regions):
        found = jnp.int32(0)
        for r in range(regions):
            found = jnp.where(spot[r] == x, r, found)
        order[x] = 2 * found + chan
        mine.append(owners[2 * found + chan])
    rank = []
    for r in range(regions):
        total = jnp.int32(0)
        for before in range(r):
            total = total + jnp.where(mine[before] == mine[r], 1, 0)
        rank.append(total)
    for r in range(regions):
        seat[r] = 2 * per_core * mine[r] + jnp.minimum(rank[r], per_core - 1)

    for copy in own:
        copy.wait()
    for at, (dy, dx, dc) in enumerate(OFFSETS):

        @pl.when(there(-dy, -dx))
        def _():
            halo(at).wait_recv()

    weights[0].wait_recv()
    top_ok, bottom_ok = (strip > 0, strip < strips - 1)
    x_ids = lax.broadcasted_iota(jnp.int32, (pwidth, 1), 0)
    x_lo = jnp.where(col > 0, 0, EDGE)
    x_hi = jnp.where(col < cols - 1, pwidth, EDGE + width)
    x_ok = (x_ids >= x_lo) & (x_ids < x_hi)

    def fill_row(y, carry):
        y_lo = jnp.where(top_ok, 0, 2)
        y_hi = jnp.where(bottom_ok, prows, prows - 2)
        ok = x_ok & (y >= y_lo) & (y < y_hi)
        for c in range(2):
            v = jnp.where(ok, pad_ref[c, y].astype(jnp.float32), 0.0)
            for b, t in enumerate(taps(v)):
                at = b * chans + c * half
                s0[pl.ds(y * pwidth, pwidth), at : at + half] = t.astype(jnp.bfloat16)
        return carry

    lax.fori_loop(0, prows, fill_row, 0, unroll=4)

    hid_rows = prows - 2
    step = 6
    size = step * pwidth
    ids = lax.broadcasted_iota(jnp.int32, (size, 1), 0)
    sub_row = ids // pwidth
    sub_col = ids % pwidth

    def hidden_chunk(i, carry):
        acc = None
        for a in range(3):
            term = dot(s0[pl.ds(pl.multiple_of((i * step + a) * pwidth, pwidth), size), :], both(t1, a))
            acc = term if acc is None else acc + term
        y = sub_row + i * step
        y_lo = jnp.where(top_ok, 0, 1)
        y_hi = jnp.where(bottom_ok, hid_rows, hid_rows - 1)
        ok = (sub_col >= x_lo) & (sub_col < x_hi) & (y >= y_lo) & (y < y_hi)
        v = jnp.where(ok, acc * sigmoid(acc), 0.0)
        for b, t in enumerate(taps(v)):
            s1[pl.ds(pl.multiple_of(i * size, size), size), b * chans : (b + 1) * chans] = t.astype(jnp.bfloat16)
        return carry

    lax.fori_loop(0, hid_rows // step, hidden_chunk, 0)

    weights[1].wait_recv()
    fstep = 8
    fsize = fstep * pwidth

    def feat_chunk(i, carry):
        acc = None
        for a in range(3):
            term = dot(s1[pl.ds(pl.multiple_of((i * fstep + a) * pwidth, pwidth), fsize), :], both(t2, a))
            acc = term if acc is None else acc + term
        v = (acc * sigmoid(acc)).reshape(fstep, pwidth, chans)[:, EDGE : EDGE + width, :]
        feat[pl.ds(pl.multiple_of(i * fstep * width, fstep * width), fstep * width), :] = v.reshape(
            fstep * width, chans
        ).astype(jnp.bfloat16)
        return carry

    lax.fori_loop(0, rows // fstep, feat_chunk, 0)

    block = samples * EDGE
    p = lax.broadcasted_iota(jnp.int32, (block, 1), 0)
    i_id, k_id = (p // EDGE, p % EDGE)
    q = lax.broadcasted_iota(jnp.int32, (1, rows * width), 1)
    y_id, x_id = (q // width, q % width)
    live = k_id < samples
    zeros = jnp.zeros((EDGE, 3 * chans), jnp.bfloat16)

    def put(dst, r, v):
        for b, t in enumerate(taps(v)):
            dst[r, EDGE : EDGE + block, b * chans : (b + 1) * chans] = t.astype(jnp.bfloat16)

    def crop_one(r, carry):
        row = sample_weight(boxes[0, order[r]] - strip * rows, boxes[2, order[r]], i_id, y_id, samples)
        column = sample_weight(boxes[1, order[r]] - col * width, boxes[3, order[r]], k_id, x_id, samples)
        weight = jnp.where(live, row * column, 0.0).astype(jnp.bfloat16)
        put(sc, r, dot(weight, feat[...]))
        for dst in (sc, sa):
            dst[r, 0:EDGE, :] = zeros
            dst[r, EDGE + block : 2 * EDGE + block, :] = zeros
        return carry

    lax.fori_loop(0, regions, crop_one, 0)

    def conv(src, g, w):
        acc = None
        for a in range(3):
            lhs = src[pl.ds(g * group, group), a * EDGE : a * EDGE + block, :].reshape(group * block, 3 * chans)
            term = dot(lhs, both(w, a))
            acc = term if acc is None else acc + term
        return acc.reshape(group, block, chans)

    weights[2].wait_recv()
    weights[3].wait_recv()

    def first_layer(g, carry):
        pre = conv(sc, g, m1)
        for n in range(group):
            v = pre[n]
            s = sigmoid(v)
            slope1[g * group + n] = s * (1.0 + v * (1.0 - s))
            put(sa, g * group + n, jnp.where(live, v * s, 0.0))
        return carry

    def second_layer(g, carry):
        pre = conv(sa, g, m2)
        for n in range(group):
            r = g * group + n
            v = pre[n]
            s = sigmoid(v)
            slope2[r] = s * (1.0 + v * (1.0 - s))
            mask_own[r] = (v * s).astype(jnp.bfloat16)
        return carry

    row_id = lax.broadcasted_iota(jnp.int32, (packed, 1), 0)
    lane_id = lax.broadcasted_iota(jnp.int32, (1, block), 1)
    for p in range(per_core):
        local = row_id - p * area
        line = (local * 4682) >> 16
        cell = line * EDGE + local - line * samples
        hit = (local >= 0) & (local < area) & (cell == lane_id)
        pack[p] = jnp.where(hit, 1.0, 0.0).astype(jnp.bfloat16)

    def gather_mask(d, carry):
        o = lax.rem(base + d, strips)
        for p in range(per_core):
            pick = jnp.int32(0)
            for r in range(regions):
                pick = jnp.where((mine[r] == o) & (rank[r] == p), r, pick)
            term = dot(pack[p], mask_own[pick])
            out = term if p == 0 else out + term
        for c in range(2):
            mask_out[2 * o + c] = out[:, c * half : (c + 1) * half].astype(jnp.bfloat16)
        for c in range(2):
            away = lax.rem(2 * o + c - me + peers, peers)

            @pl.when(away > 0)
            def _():
                block_copy(mask_out, mask_got, mask_send, mask_recv, away).start()

        return carry

    groups = regions // group

    def layers(g, carry):
        first_layer(g, carry)
        second_layer(g, carry)
        done = jnp.where(g == groups - 1, strips, jnp.minimum((g + 1) * group // per_core, strips - 1))
        lax.fori_loop(jnp.minimum(g * group // per_core, strips - 1), done, gather_mask, 0)
        return carry

    lax.fori_loop(0, groups, layers, 0)
    mask_got[me] = mask_out[me]

    def wait_cot(d, carry):
        block_copy(cot_out, cot_got, cot_send, cot_recv, d).wait()
        return carry

    lax.fori_loop(1, peers, wait_cot, 0)

    yt = lax.broadcasted_iota(jnp.int32, (rows * width, 1), 0)
    yt_id, xt_id = (yt // width, yt % width)
    pt = lax.broadcasted_iota(jnp.int32, (1, block), 1)
    it_id, kt_id = (pt // EDGE, pt % EDGE)

    packed_id = lax.broadcasted_iota(jnp.int32, (1, packed), 1)

    def start_grad(r, carry):
        at_seat = seat[r]
        owner = at_seat // (2 * per_core)
        place = lax.rem(at_seat, 2 * per_core)
        taken = place * area + i_id * samples + k_id
        spread = jnp.where(live & (taken == packed_id), 1.0, 0.0).astype(jnp.bfloat16)
        cot = dot(spread, jnp.concatenate([cot_got[2 * owner], cot_got[2 * owner + 1]], axis=-1))
        put(sc, r, cot * slope2[r])
        row = sample_weight(
            boxes[0, order[r]] - strip * rows, boxes[2, order[r]], it_id, yt_id, samples
        )
        column = sample_weight(
            boxes[1, order[r]] - col * width, boxes[3, order[r]], kt_id, xt_id, samples
        )
        mt[r] = jnp.where(kt_id < samples, row * column, 0.0).astype(jnp.bfloat16)
        return carry

    lax.fori_loop(0, regions, start_grad, 0)

    def back(src, g, w):
        acc = None
        for a in range(3):
            for b in range(3):
                lhs = src[
                    pl.ds(g * group, group), a * EDGE : a * EDGE + block, b * chans : (b + 1) * chans
                ].reshape(group * block, chans)
                term = dot_t(lhs, both(w, 2 - a, slice((2 - b) * chans, (3 - b) * chans)))
                acc = term if acc is None else acc + term
        return acc.reshape(group, block, chans)

    def second_back(g, carry):
        d = back(sc, g, m2)
        for n in range(group):
            r = g * group + n
            put(sa, r, jnp.where(live, d[n] * slope1[r], 0.0))
        return carry

    lax.fori_loop(0, regions // group, second_back, 0)

    def first_back(g, carry):
        d = back(sa, g, m1)
        for n in range(group):
            cg[g * group + n] = d[n].astype(jnp.bfloat16)
        return carry

    lax.fori_loop(0, regions // group, first_back, 0)

    total = None
    for r in range(regions):
        term = dot(mt[r], cg[r])
        total = term if total is None else total + term
    for c in range(2):
        part[c] = total[:, c * half : (c + 1) * half]
    sum_copy = pltpu.make_async_remote_copy(
        src_ref=part.at[1 - chan],
        dst_ref=part_got,
        send_sem=part_sem.at[0],
        recv_sem=part_sem.at[1],
        device_id=near(0, 0, 1),
        device_id_type=MESH,
    )
    sum_copy.start()

    def wait_mask(d, carry):
        block_copy(mask_out, mask_got, mask_send, mask_recv, d).wait()
        return carry

    lax.fori_loop(1, peers, wait_mask, 0)

    def place_one(n, carry):
        def look(at, found):
            return jnp.where(table[at] == n, at, found)

        at = lax.fori_loop(0, peers * per_core, look, jnp.int32(-1))
        at0 = jnp.maximum(at, 0)
        got = mask_got[at0 // per_core, 0:area, :]
        for p in range(1, per_core):
            got = jnp.where(at0 % per_core == p, mask_got[at0 // per_core, p * area : (p + 1) * area, :], got)
        mask_ref[n] = jnp.where(at >= 0, got, jnp.zeros_like(got))
        return carry

    lax.fori_loop(0, capacity, place_one, 0)
    sum_copy.wait()
    grad_ref[...] = (part[chan] + part_got[...]).reshape(rows, width, half).astype(grad_ref.dtype)
    for at, (dy, dx, dc) in enumerate(OFFSETS):

        @pl.when(there(dy, dx))
        def _():
            halo(at).wait_send()

    for copy in weights:
        copy.wait_send()


def shards(
    features, tile_first, tile_second, mask_first, mask_second, region_boxes, owner_strip, cotangent
):
    rows, width, half = features.shape
    chans = 2 * half
    capacity, samples = (cotangent.shape[2], cotangent.shape[3])
    block = samples * EDGE
    strips, cols = (lax.axis_size("strip"), lax.axis_size("col"))
    slots = owner_strip.shape[2]
    regions = slots // 2
    per_core = -(-(-(-capacity // strips)) // 2)
    peers = 2 * strips
    prows, pwidth = (rows + 4, width + 2 * EDGE)
    group = 2
    vmem = pl.BlockSpec(memory_space=pltpu.VMEM)
    smem = pl.BlockSpec(memory_space=pltpu.SMEM)
    weights = [w.reshape(3, 3 * chans, half) for w in (tile_first, tile_second, mask_first, mask_second)]
    bf16, f32, i32 = (jnp.bfloat16, jnp.float32, jnp.int32)
    sem = pltpu.SemaphoreType.DMA
    area = samples * samples
    packed = -(-per_core * area // EDGE) * EDGE
    blocks = pltpu.VMEM((peers, packed, half), bf16)
    stack = pltpu.VMEM((regions, block + 2 * EDGE, 3 * chans), bf16)
    slope = pltpu.VMEM((regions, block, chans), f32)
    mask_out, grad_tile = pl.pallas_call(
        functools.partial(head_kernel, strips, cols, group, samples),
        out_shape=[
            jax.ShapeDtypeStruct((capacity, area, half), bf16),
            jax.ShapeDtypeStruct((rows, width, half), bf16),
        ],
        in_specs=[smem, smem, vmem, vmem] + [pl.BlockSpec(memory_space=pl.ANY)] * 4 + [vmem],
        out_specs=[vmem, vmem],
        scratch_shapes=[pltpu.VMEM((2, prows, pwidth, half), bf16)]
        + [pltpu.VMEM((2, 3, 3 * chans, half), bf16)] * 4
        + [
            pltpu.VMEM((8, 128), i32),
            pltpu.VMEM((strips, 8, 128), i32),
            pltpu.SMEM((strips, 8, 128), i32),
            pltpu.SMEM((peers * per_core,), i32),
            pltpu.SMEM((regions,), i32),
            pltpu.SMEM((regions,), i32),
        ]
        + [blocks] * 4
        + [
            pltpu.VMEM((2, rows * width, half), f32),
            pltpu.VMEM((rows * width, half), f32),
            pltpu.VMEM((prows * pwidth, 3 * chans), bf16),
            pltpu.VMEM(((prows - 2) * pwidth, 3 * chans), bf16),
            pltpu.VMEM((rows * width, chans), bf16),
            stack,
            stack,
            slope,
            slope,
            pltpu.VMEM((regions, block, chans), bf16),
            pltpu.VMEM((per_core, packed, block), bf16),
            pltpu.VMEM((regions, rows * width, block), bf16),
            pltpu.VMEM((regions, block, chans), bf16),
        ]
        + [sem((len(OFFSETS),))] * 2
        + [sem((4,))] * 2
        + [sem((strips,))] * 2
        + [sem((peers,))] * 4
        + [sem((2,)), sem((6,))],
        compiler_params=pltpu.CompilerParams(
            collective_id=0, has_side_effects=True, vmem_limit_bytes=VMEM_BYTES
        ),
        name="head",
    )(region_boxes[0, 0].T, owner_strip[0, 0], owner_strip[0], features, *weights, cotangent.reshape(capacity, area, half))
    return (mask_out.reshape(cotangent.shape), grad_tile)


def solution(mesh):
    placed = (
        P(("grp", "strip"), "col", "chan"),
        P(None, None, None, "chan"),
        P(None, None, None, "chan"),
        P(None, None, None, "chan"),
        P(None, None, None, "chan"),
        P(("grp", "strip"), "col", None, None),
        P(("grp", "strip"), "col", None),
        P(("grp", "strip"), "col", None, None, None, "chan"),
    )
    return jax.shard_map(
        shards,
        mesh=mesh,
        in_specs=placed,
        out_specs=(
            P(("grp", "strip"), "col", None, None, None, "chan"),
            P(("grp", "strip"), "col", "chan"),
        ),
        check_vma=False,
    )
```
